256 devices in a mesh: row: 16 (over z, core), col: 16 (over x, y).
Axes of the slice: x: 4, y: 4, z: 8, core: 2. Of those that a mesh axis runs over, the one named last changes fastest.
Arguments:
- density: bfloat16 [2, 6144, 6144], P(None, 'row', 'col'), as said below
- weighted: bfloat16 [6144, 6144], P('row', 'col'), as said below
- ham_deriv: bfloat16 [3, 6144, 6144], P(None, 'row', 'col'), may hold values from -0.1875 to 0.1875
- ovl_deriv: bfloat16 [3, 6144, 6144], P(None, 'row', 'col'), may hold values from -0.1875 to 0.1875
- tile_pattern: int32 [48, 48], P('row', 'col'), may hold values from 0 to 1, as said below
- branch: int32 [2], replicated, may hold values from 0 to 1, each once
- orbital_atom: int32 [16, 384], P('row'), may hold values from 0 to 95, never falling along the last dimension, each value on 1 to 9 neighbouring positions
- positions: float32 [3, 1536], P(None, 'row'), may hold values from -6 to 6
- velocities: float32 [3, 1536], P(None, 'row'), may hold values from -12 to 12
- masses: float32 [1536], P('row'), may hold values from 0.4 to 33
Outputs:
- purified: bfloat16 [2, 6144, 6144], P(None, 'row', 'col')
- forces: float32 [3, 1536], P(None, 'row')
- new_velocities: float32 [3, 1536], P(None, 'row')
- new_positions: float32 [3, 1536], P(None, 'row')
The draws below stay inside these ranges and needn't reach their ends.
Inputs may be any that keep to these rules, and one draw needn't show every extreme that they name: `orbital_atom`: in each slab the atom numbers never fall and every atom has 1 to 9 orbitals. `tile_pattern`: the pattern is symmetric, and every diagonal block lies on it. `density`: each channel's matrix is symmetric and zero on every block where tile_pattern is 0. `weighted`: symmetric and zero on every block where tile_pattern is 0. `branch`: the two spin channels take different branches.
All inputs are finite; a program needn't handle non-finite values.
Results may differ from the reference program's by a relative error of at most 0.01.
Values may be sent and summed in bfloat16 or wider, within the bound.
No kernel may reach another device: no remote copies, remote signals or barrier semaphores. Data moves between devices by JAX's collectives and lax.ppermute only.
A program may use at most 64 MiB of HBM per device.

```python
import math
import jax
import jax.numpy as jnp
import numpy as np
from jax import lax

TILE = 128
SPINS = 2
MOST_ORB = 9
ROWS = 384
ORDER = 6144
BLOCKS = 48
ATOMS_SLAB = 96
ATOMS = 1536
N_ROW = 16


def block_mask(key):
    upper = jax.random.randint(key, (BLOCKS, BLOCKS), 0, 4) < 3
    rows = jnp.arange(BLOCKS, dtype=jnp.int32)[:, None]
    cols = jnp.arange(BLOCKS, dtype=jnp.int32)[None, :]
    mirrored = jnp.where(rows <= cols, upper, upper.T)
    return jnp.where(rows == cols, True, mirrored).astype(jnp.int32)


def mirror_on_pattern(values, pattern, scale):
    mirrored = (values + jnp.swapaxes(values, -1, -2)) * 0.5 ** 0.5 * scale
    lead = mirrored.shape[:-2]
    shaped = mirrored.reshape(lead + (BLOCKS, TILE, BLOCKS, TILE))
    weights = pattern.astype(jnp.float32)[:, None, :, None]
    return (shaped * weights).reshape(mirrored.shape).astype(jnp.bfloat16)


def draw_tile_pattern(key, part):
    return block_mask(key)


def draw_density(key, part):
    pattern = block_mask(key)
    key = jax.random.fold_in(key, 5)
    values = jnp.clip(jax.random.normal(key, (SPINS, ORDER, ORDER), jnp.float32), -4.0, 4.0)
    return mirror_on_pattern(values, pattern, ORDER ** (-0.25))


def draw_weighted(key, part):
    pattern = block_mask(key)
    key = jax.random.fold_in(key, 7)
    values = jnp.clip(jax.random.normal(key, (ORDER, ORDER), jnp.float32), -4.0, 4.0)
    return mirror_on_pattern(values, pattern, 1.0)


def draw_masses(key, part):
    key = jax.random.fold_in(key, 11)
    ramp = jnp.arange(ATOMS, dtype=jnp.float32) / ATOMS
    factor = jnp.exp(jax.random.uniform(key, (ATOMS,), jnp.float32, -1.0, 1.0))
    return 12.0 * factor * jnp.power(9.0, -ramp)


def draw_velocities(key, part):
    key = jax.random.fold_in(key, 23)
    ramp = jnp.arange(ATOMS, dtype=jnp.float32) / ATOMS
    values = jnp.clip(jax.random.normal(key, (3, ATOMS), jnp.float32), -4.0, 4.0)
    return values * jnp.power(3.0, ramp)[None, :]


def level_of(stream_key, dims, cuts, smallest, high):
    def one(dim, parts):
        draws = jax.random.uniform(jax.random.fold_in(jax.random.fold_in(stream_key, 6), dim), (parts,), jnp.float32, smallest / len(cuts), high / len(cuts))
        return jnp.repeat(jnp.exp(draws), dims[dim] // parts).reshape((-1,) + (1,) * (len(dims) - dim - 1))

    level = one(*cuts[0])
    for cut in cuts[1:]:
        level = level * one(*cut)
    return level


def length_profile(count, total, reach, slope):
    weights = [(1 << 20) // math.isqrt(rank ** slope) + 1 for rank in range(2, count + 1)]
    spare, counts = total - reach - (count - 1), [1] * (count - 1)
    while spare > 0:
        candidates = [i for i in range(count - 1) if counts[i] < reach]
        pool, remaining = sum([weights[i] for i in candidates]), spare
        for i in candidates:
            extra = min(reach - counts[i], max(1, remaining * weights[i] // pool), spare)
            counts[i] = counts[i] + extra
            spare = spare - extra
    return np.array([reach] + counts)


def ragged_sizes(own_key, count, total, most, skew):
    if count == 2:
        one = jax.random.randint(own_key, (), max(1, total - most), min(most, total - 1) + 1)
        return jnp.stack([one, total - one])
    sizes = jnp.asarray(length_profile(count, total, most, skew), jnp.int32)
    pairs = (count - 1) // 2
    source_of, receiver = sizes[1:1 + 2 * pairs:2], sizes[2:2 + 2 * pairs:2]
    margin = jnp.minimum(source_of - 1, most - receiver)
    moved = jax.random.randint(jax.random.fold_in(own_key, 1), (pairs,), 0, 1 << 20) % (margin + 1)
    sizes = sizes.at[1:1 + 2 * pairs:2].set(source_of - moved).at[2:2 + 2 * pairs:2].set(receiver + moved)
    return sizes[jax.random.permutation(jax.random.fold_in(own_key, 2), count)]


def centred(stream_key, extent, width, reach, split=(), kind=jnp.bfloat16):
    drawn = width * jax.random.normal(stream_key, extent, jnp.float32)
    if split:
        drawn = drawn * level_of(stream_key, extent, split, -0.22, 0.18)
    return jnp.clip(drawn, -reach, reach).astype(kind)


def setup_inputs(seed: int = 0) -> dict:
    keys = jax.random.split(jax.random.key(seed), 11)
    return {
        "density": draw_density(jax.random.fold_in(keys[10], 71), 0),
        "weighted": draw_weighted(jax.random.fold_in(keys[10], 71), 0),
        "ham_deriv": centred(keys[2], (3, ORDER, ORDER), (ORDER ** -0.5), 0.1875, ((1, 16), (2, 16))),
        "ovl_deriv": centred(keys[3], (3, ORDER, ORDER), (ORDER ** -0.5), 0.1875, ((1, 16), (2, 16))),
        "tile_pattern": draw_tile_pattern(jax.random.fold_in(keys[10], 71), 0),
        "branch": jax.random.permutation(keys[5], SPINS).astype(jnp.int32),
        "orbital_atom": jax.vmap(lambda own: jnp.searchsorted(jnp.cumsum(ragged_sizes(own, ATOMS_SLAB, ROWS, MOST_ORB, 0)), jnp.arange(ROWS), side="right"))(jax.random.split(keys[6], N_ROW)).reshape((N_ROW, ROWS)).astype(jnp.int32),
        "positions": centred(keys[7], (3, ATOMS), 1.0, 6.0, ((1, 16),), jnp.float32),
        "velocities": draw_velocities(jax.random.fold_in(keys[10], 71), 0),
        "masses": draw_masses(jax.random.fold_in(keys[10], 71), 0),
    }


mixing = 0.25
time_step = 0.1
epsilon = 1e-06

def on_pattern(matrix, tile_pattern):
    lead = matrix.shape[:-2]
    shaped = matrix.reshape(lead + (BLOCKS, TILE, BLOCKS, TILE))
    pattern = tile_pattern.astype(matrix.dtype)[:, None, :, None]
    return (shaped * pattern).reshape(matrix.shape)

def reference(density, weighted, ham_deriv, ovl_deriv, tile_pattern, branch, orbital_atom, positions, velocities, masses):
    square = jnp.stack([jnp.dot(density[spin], density[spin], preferred_element_type=jnp.float32) for spin in range(SPINS)])
    flip = (branch == 1)[:, None, None]
    raw = jnp.where(flip, 2.0 * density.astype(jnp.float32) - square, square)
    purified = on_pattern(raw, tile_pattern).astype(jnp.bfloat16)
    purified_wide = purified.astype(jnp.float32)
    weight_wide = weighted.astype(jnp.float32)
    terms = []
    for direction in range(3):
        first = lax.optimization_barrier(jnp.sum(purified_wide * ham_deriv[direction].astype(jnp.float32)[None, :, :], axis=(0, 2)))
        second = lax.optimization_barrier(jnp.sum(weight_wide * ovl_deriv[direction].astype(jnp.float32), axis=1))
        terms.append(first - second)
    orbital_terms = jnp.stack(terms).reshape(3, N_ROW, ROWS)
    one_hot = (orbital_atom[:, :, None] == jnp.arange(ATOMS_SLAB, dtype=jnp.int32)[None, None, :]).astype(jnp.float32)
    forces = -2.0 * jnp.einsum('xrm,rma->xra', orbital_terms, one_hot, precision=lax.Precision.HIGHEST)
    forces = forces.reshape(3, ATOMS)
    root_mass = jnp.sqrt(masses)[None, :]
    scaled = forces / root_mass
    force_norm = jnp.sum(scaled * scaled)
    speed_norm = jnp.sum(velocities * velocities)
    new_velocities = (1.0 - mixing) * velocities + mixing * jnp.sqrt(speed_norm) * scaled / jnp.sqrt(force_norm + epsilon) + time_step * scaled
    new_positions = positions + time_step * new_velocities / root_mass
    return (purified, forces, new_velocities, new_positions)
```

```python
import jax
import jax.numpy as jnp
from jax import lax
from jax.experimental import pallas as pl
from jax.experimental.pallas import tpu as pltpu
from jax.sharding import PartitionSpec as P

TILE = 128
ROWS = 384
SLABS = 16
LANES = 128

mixing = 0.25
time_step = 0.1
epsilon = 1e-06

AXES = ("row", "col")


def place(z, core, x, y):
    return (z % 8 * 2 + core) * 16 + x % 4 * 4 + y % 4


def pairs(move):
    out = []
    for z in range(8):
        for core in range(2):
            for x in range(4):
                for y in range(4):
                    out.append((place(z, core, x, y), place(*move(z, core, x, y))))
    return out


def x_by(k):
    return pairs(lambda z, core, x, y: (z, core, x + k, y))


def y_by(k):
    return pairs(lambda z, core, x, y: (z, core, x, y + k))


def z_by(k):
    return pairs(lambda z, core, x, y: (z + k, core, x, y))


def z_swap():
    return pairs(lambda z, core, x, y: (z ^ 1, core, x, y))


def core_swap():
    return pairs(lambda z, core, x, y: (z, 1 - core, x, y))


def send(value, table):
    return lax.ppermute(value, AXES, table)


def gather_plane(block, first, second):
    one = send(block, first(1))
    two = send(block, first(-1))
    three = send(block, first(2))
    line = jnp.stack([block, one, two, three])
    ahead = send(line, second(1))
    behind = send(line, second(-1))
    far_low = send(ahead[:2], second(1))
    far_high = send(behind[2:], second(-1))
    return (line, ahead, behind, far_low, far_high)


def slots(first_at, second_at):
    line = [0, -1, 1, 2]
    order = [(a, 0) for a in line] + [(a, -1) for a in line] + [(a, 1) for a in line]
    order += [(a, 2) for a in line]
    return [((first_at + a) & 3, (second_at + b) & 3) for a, b in order]


def terms_of(matrix, deriv_ref, one_hot):
    rows = []
    for x in range(3):
        column = jnp.sum(matrix * deriv_ref[x].astype(jnp.float32), axis=1, keepdims=True)
        rows.append(jnp.sum(column * one_hot, axis=0, keepdims=True))
    return rows


def one_hot_of(atom_ref):
    lanes = lax.broadcasted_iota(jnp.int32, (ROWS, LANES), 1)
    return (atom_ref[...] == lanes).astype(jnp.float32)


def overlap_kernel(atom_ref, weighted_ref, ovl_ref, out_ref):
    rows = terms_of(weighted_ref[...].astype(jnp.float32), ovl_ref, one_hot_of(atom_ref))
    out_ref[...] = jnp.zeros_like(out_ref)
    for x in range(3):
        out_ref[x : x + 1, :] = 2.0 * rows[x]


PIECES = (4, 4, 4, 2, 2)
PARTS = 4


def purify(spin, slab_ref, branch_ref, pattern_ref, own_ref, pieces, b_ref, a_buf, b_buf, sems, total):
    copies = []
    t = 0
    for piece, count in zip(pieces, PIECES):
        for i in range(count):
            a_copy = pltpu.make_async_copy(
                piece.at[i], a_buf.at[:, pl.ds(t * ROWS, ROWS)], sems.at[0, t]
            )
            start = pl.multiple_of(slab_ref[t] * ROWS, ROWS)
            b_copy = pltpu.make_async_copy(
                b_ref.at[pl.ds(start, ROWS), :], b_buf.at[pl.ds(t * ROWS, ROWS), :], sems.at[1, t]
            )
            a_copy.start()
            b_copy.start()
            copies.append((a_copy, b_copy))
            t += 1
    each = SLABS // PARTS
    for part in range(PARTS):
        for a_copy, b_copy in copies[part * each : (part + 1) * each]:
            a_copy.wait()
            b_copy.wait()
        ks = pl.ds(part * each * ROWS, each * ROWS)
        product = jnp.dot(a_buf[:, ks], b_buf[ks, :], preferred_element_type=jnp.float32)
        if part == 0:
            total[...] = product
        else:
            total[...] += product
    square = total[...]
    flip = branch_ref[spin] == 1
    raw = jnp.where(flip, 2.0 * own_ref[...].astype(jnp.float32) - square, square)
    blocks = []
    for i in range(3):
        row = []
        for j in range(3):
            weight = pattern_ref[i, j].astype(jnp.float32)
            row.append(raw[i * TILE : (i + 1) * TILE, j * TILE : (j + 1) * TILE] * weight)
        blocks.append(jnp.concatenate(row, axis=1))
    return jnp.concatenate(blocks, axis=0).astype(jnp.bfloat16)


def first_kernel(slab_ref, branch_ref, pattern_ref, own_ref, *rest):
    pieces, (b_ref, out_ref, a_buf, b_buf, sems, total) = rest[:5], rest[5:]
    out_ref[...] = purify(
        0, slab_ref, branch_ref, pattern_ref, own_ref, pieces, b_ref, a_buf, b_buf, sems, total
    )


def second_kernel(slab_ref, branch_ref, pattern_ref, own_ref, *rest):
    pieces, rest = rest[:5], rest[5:]
    b_ref, other_ref, atom_ref, ham_ref, overlap_ref, out_ref, sums_ref = rest[:7]
    a_buf, b_buf, sems, total = rest[7:]
    purified = purify(
        1, slab_ref, branch_ref, pattern_ref, own_ref, pieces, b_ref, a_buf, b_buf, sems, total
    )
    out_ref[...] = purified
    both = purified.astype(jnp.float32) + other_ref[...].astype(jnp.float32)
    rows = terms_of(both, ham_ref, one_hot_of(atom_ref))
    sums_ref[...] = overlap_ref[...]
    for x in range(3):
        sums_ref[x : x + 1, :] += -2.0 * rows[x]


SMEM = pl.BlockSpec(memory_space=pltpu.SMEM)
VMEM = pl.BlockSpec(memory_space=pltpu.VMEM)
ANY = pl.BlockSpec(memory_space=pl.ANY)


def scratch():
    return [
        pltpu.VMEM((ROWS, SLABS * ROWS), jnp.bfloat16),
        pltpu.VMEM((SLABS * ROWS, ROWS), jnp.bfloat16),
        pltpu.SemaphoreType.DMA((2, SLABS)),
        pltpu.VMEM((ROWS, ROWS), jnp.float32),
    ]


COST = pl.CostEstimate(
    flops=2 * ROWS * ROWS * ROWS * SLABS,
    bytes_accessed=4 * ROWS * ROWS * SLABS,
    transcendentals=0,
)
PARAMS = pltpu.CompilerParams(vmem_limit_bytes=40 * 1024 * 1024)


def sum_of_four(value, by):
    one, two, three = send(value, by(1)), send(value, by(2)), send(value, by(3))
    return (value + two) + (one + three)


def local(
    density,
    weighted,
    ham_deriv,
    ovl_deriv,
    tile_pattern,
    branch,
    orbital_atom,
    positions,
    velocities,
    masses,
):
    column = lax.axis_index("col")
    at_x, at_y = column >> 2, column & 3
    slab_zero = jnp.stack([a * 1 + b * 4 for a, b in slots(at_y, at_x)]).astype(jnp.int32)
    slab_one = jnp.stack([a * 4 + b * 1 for a, b in slots(at_x, at_y)]).astype(jnp.int32)

    tall = [lax.all_gather(density[s], "row", axis=0, tiled=True) for s in range(2)]
    wide_zero = gather_plane(density[0], y_by, x_by)
    wide_one = gather_plane(density[1], x_by, y_by)

    atom_column = orbital_atom.reshape(ROWS, 1)
    overlap = pl.pallas_call(
        overlap_kernel,
        out_shape=jax.ShapeDtypeStruct((8, LANES), jnp.float32),
        in_specs=[VMEM] * 3,
        out_specs=VMEM,
    )(atom_column, weighted, ovl_deriv)

    purified_zero = pl.pallas_call(
        first_kernel,
        out_shape=jax.ShapeDtypeStruct((ROWS, ROWS), jnp.bfloat16),
        in_specs=[SMEM, SMEM, SMEM, VMEM] + [ANY] * 6,
        out_specs=VMEM,
        scratch_shapes=scratch(),
        compiler_params=PARAMS,
        cost_estimate=COST,
    )(slab_zero, branch, tile_pattern, density[0], *wide_zero, tall[0])

    purified_one, sums = pl.pallas_call(
        second_kernel,
        out_shape=(
            jax.ShapeDtypeStruct((ROWS, ROWS), jnp.bfloat16),
            jax.ShapeDtypeStruct((8, LANES), jnp.float32),
        ),
        in_specs=[SMEM, SMEM, SMEM, VMEM] + [ANY] * 6 + [VMEM] * 4,
        out_specs=(VMEM, VMEM),
        scratch_shapes=scratch(),
        compiler_params=PARAMS,
        cost_estimate=COST,
    )(
        slab_one,
        branch,
        tile_pattern,
        density[1],
        *wide_one,
        tall[1],
        purified_zero,
        atom_column,
        ham_deriv,
        overlap,
    )
    purified = jnp.stack([purified_zero, purified_one])

    sums = sum_of_four(sums, x_by)
    sums = sum_of_four(sums, y_by)
    forces = sums[:3, : positions.shape[1]]

    root_mass = jnp.sqrt(masses)[None, :]
    scaled = forces / root_mass
    norms = jnp.stack([jnp.sum(scaled * scaled), jnp.sum(velocities * velocities)])
    norms = jnp.broadcast_to(norms[:, None], (2, LANES))
    norms = norms + send(norms, core_swap())
    norms = norms + send(norms, z_swap())
    two, four, six = send(norms, z_by(2)), send(norms, z_by(4)), send(norms, z_by(6))
    norms = (norms + four) + (two + six)
    force_norm, speed_norm = norms[0, 0], norms[1, 0]
    new_velocities = (
        (1.0 - mixing) * velocities
        + mixing * jnp.sqrt(speed_norm) * scaled / jnp.sqrt(force_norm + epsilon)
        + time_step * scaled
    )
    new_positions = positions + time_step * new_velocities / root_mass
    return (purified, forces, new_velocities, new_positions)


def solution(mesh):
    in_specs = (
        P(None, "row", "col"),
        P("row", "col"),
        P(None, "row", "col"),
        P(None, "row", "col"),
        P("row", "col"),
        P(),
        P("row", None),
        P(None, "row"),
        P(None, "row"),
        P("row"),
    )
    out_specs = (P(None, "row", "col"), P(None, "row"), P(None, "row"), P(None, "row"))
    return jax.shard_map(local, mesh=mesh, in_specs=in_specs, out_specs=out_specs, check_vma=False)
```

```python
import jax
import jax.numpy as jnp
from jax import lax
from jax.experimental import pallas as pl
from jax.experimental.pallas import tpu as pltpu
from jax.sharding import PartitionSpec as P

TILE = 128
ROWS = 384
SLABS = 16
LANES = 128

mixing = 0.25
time_step = 0.1
epsilon = 1e-06

AXES = ("row", "col")


def place(z, core, x, y):
    return (z % 8 * 2 + core) * 16 + x % 4 * 4 + y % 4


def pairs(move):
    out = []
    for z in range(8):
        for core in range(2):
            for x in range(4):
                for y in range(4):
                    out.append((place(z, core, x, y), place(*move(z, core, x, y))))
    return out


def x_by(k):
    return pairs(lambda z, core, x, y: (z, core, x + k, y))


def y_by(k):
    return pairs(lambda z, core, x, y: (z, core, x, y + k))


def x_swap(bit):
    return pairs(lambda z, core, x, y: (z, core, x ^ bit, y))


def y_swap(bit):
    return pairs(lambda z, core, x, y: (z, core, x, y ^ bit))


def z_swap(bit):
    return pairs(lambda z, core, x, y: (z ^ bit, core, x, y))


def core_swap():
    return pairs(lambda z, core, x, y: (z, 1 - core, x, y))


def send(value, table):
    return lax.ppermute(value, AXES, table)


def gather_plane(block, first, second):
    one = send(block, first(1))
    two = send(block, first(-1))
    three = send(block, first(2))
    near = jnp.stack([block, one])
    ahead_near = send(near, second(1))
    behind_near = send(near, second(-1))
    rest = jnp.stack([two, three])
    ahead_rest = send(rest, second(1))
    behind_rest = send(rest, second(-1))
    far_near = send(ahead_near, second(1))
    far_rest = send(behind_rest, second(-1))
    return (near, ahead_near, behind_near, far_near, rest, ahead_rest, behind_rest, far_rest)


def slots(first_at, second_at):
    order = [(a, b) for line in ((0, -1), (1, 2)) for b in (0, -1, 1, 2) for a in line]
    return [((first_at + a) & 3, (second_at + b) & 3) for a, b in order]


def terms_of(matrix, deriv_ref, one_hot):
    rows = []
    for x in range(3):
        column = jnp.sum(matrix * deriv_ref[x].astype(jnp.float32), axis=1, keepdims=True)
        rows.append(jnp.sum(column * one_hot, axis=0, keepdims=True))
    return rows


def one_hot_of(atom_ref):
    lanes = lax.broadcasted_iota(jnp.int32, (ROWS, LANES), 1)
    return (atom_ref[...] == lanes).astype(jnp.float32)


def overlap_kernel(atom_ref, weighted_ref, ovl_ref, out_ref):
    rows = terms_of(weighted_ref[...].astype(jnp.float32), ovl_ref, one_hot_of(atom_ref))
    out_ref[...] = jnp.zeros_like(out_ref)
    for x in range(3):
        out_ref[x : x + 1, :] = 2.0 * rows[x]


PIECES = 8
GROUPS = 4


def b_copies(facts_ref, tall_ref, b_buf, sems):
    copies = []
    for spin in range(2):
        for t in range(SLABS):
            start = pl.multiple_of(facts_ref[spin * SLABS + t] * ROWS, ROWS)
            copies.append(
                pltpu.make_async_copy(
                    tall_ref.at[spin, pl.ds(start, ROWS), :],
                    b_buf.at[spin, pl.ds(t * ROWS, ROWS), :],
                    sems.at[spin, t],
                )
            )
    return copies


def purify_kernel(facts_ref, *rest):
    wide = (rest[:PIECES], rest[PIECES : 2 * PIECES])
    tall_ref, density_ref, deriv_ref, atom_ref, overlap_ref = rest[2 * PIECES : 2 * PIECES + 5]
    out_ref, sums_ref, b_buf, sems, total, own_ref, ham_ref, own_sems = rest[2 * PIECES + 5 :]
    copies = b_copies(facts_ref, tall_ref, b_buf, sems)
    own_copy = pltpu.make_async_copy(density_ref, own_ref, own_sems.at[0])
    ham_copy = pltpu.make_async_copy(deriv_ref, ham_ref, own_sems.at[1])
    for copy in copies[:SLABS]:
        copy.start()
    own_copy.start()
    for copy in copies[SLABS:]:
        copy.start()
    ham_copy.start()
    each = SLABS // GROUPS
    for spin in range(2):
        for group in range(GROUPS):
            for copy in copies[spin * SLABS + group * each : spin * SLABS + (group + 1) * each]:
                copy.wait()
            slabs = [wide[spin][group * each // 2 + i][j] for i in range(each // 2) for j in range(2)]
            product = jnp.dot(
                jnp.concatenate(slabs, axis=1),
                b_buf[spin, pl.ds(group * each * ROWS, each * ROWS), :],
                preferred_element_type=jnp.float32,
            )
            if group == 0:
                total[...] = product
            else:
                total[...] += product
        square = total[...]
        if spin == 0:
            own_copy.wait()
        flip = facts_ref[2 * SLABS + spin] == 1
        raw = jnp.where(flip, 2.0 * own_ref[spin].astype(jnp.float32) - square, square)
        for i in range(3):
            for j in range(3):
                weight = facts_ref[2 * SLABS + 2 + 3 * i + j].astype(jnp.float32)
                at = (slice(i * TILE, (i + 1) * TILE), slice(j * TILE, (j + 1) * TILE))
                out_ref[(spin,) + at] = (raw[at] * weight).astype(jnp.bfloat16)
    both = out_ref[0].astype(jnp.float32) + out_ref[1].astype(jnp.float32)
    ham_copy.wait()
    rows = terms_of(both, ham_ref, one_hot_of(atom_ref))
    sums_ref[...] = overlap_ref[...]
    for x in range(3):
        sums_ref[x : x + 1, :] += -2.0 * rows[x]


def norm_kernel(one_ref, two_ref, velocities_ref, masses_ref, forces_ref, sums_ref, norms_ref):
    sums = one_ref[...] + two_ref[...]
    forces = sums[:3, : forces_ref.shape[1]]
    forces_ref[...] = forces
    sums_ref[...] = sums
    scaled = forces / jnp.sqrt(masses_ref[...])
    speeds = velocities_ref[...]
    rows = lax.broadcasted_iota(jnp.int32, norms_ref.shape, 0)
    norms_ref[...] = jnp.where(rows == 0, jnp.sum(scaled * scaled), jnp.sum(speeds * speeds))


def update_kernel(
    one_ref, two_ref, sums_ref, positions_ref, velocities_ref, masses_ref, speeds_ref, places_ref
):
    norms = one_ref[...] + two_ref[...]
    force_norm, speed_norm = norms[0:1, 0:1], norms[1:2, 0:1]
    root_mass = jnp.sqrt(masses_ref[...])
    scaled = sums_ref[:3, : speeds_ref.shape[1]] / root_mass
    speeds = (
        (1.0 - mixing) * velocities_ref[...]
        + mixing * jnp.sqrt(speed_norm) * scaled / jnp.sqrt(force_norm + epsilon)
        + time_step * scaled
    )
    speeds_ref[...] = speeds
    places_ref[...] = positions_ref[...] + time_step * speeds / root_mass


SMEM = pl.BlockSpec(memory_space=pltpu.SMEM)
VMEM = pl.BlockSpec(memory_space=pltpu.VMEM)
HBM = pl.BlockSpec(memory_space=pltpu.HBM)

COST = pl.CostEstimate(
    flops=4 * ROWS * ROWS * ROWS * SLABS,
    bytes_accessed=8 * ROWS * ROWS * SLABS,
    transcendentals=0,
)
PARAMS = pltpu.CompilerParams(vmem_limit_bytes=45 * 1024 * 1024)


def small(shape):
    return jax.ShapeDtypeStruct(shape, jnp.float32)


def local(
    density,
    weighted,
    ham_deriv,
    ovl_deriv,
    tile_pattern,
    branch,
    orbital_atom,
    positions,
    velocities,
    masses,
):
    column = lax.axis_index("col")
    at_x, at_y = column >> 2, column & 3
    slabs = jnp.stack(
        [
            jnp.stack([a + b * 4 for a, b in slots(at_y, at_x)]),
            jnp.stack([a * 4 + b for a, b in slots(at_x, at_y)]),
        ]
    ).astype(jnp.int32)
    facts = jnp.concatenate([slabs.reshape(-1), branch, tile_pattern.reshape(-1)])

    tall = lax.all_gather(density, "row", axis=1, tiled=True)
    low, high = lax.optimization_barrier((density[0], density[1]))
    wide_zero = gather_plane(low, y_by, x_by)
    wide_one = gather_plane(high, x_by, y_by)

    atom_column = orbital_atom.reshape(ROWS, 1)
    overlap = pl.pallas_call(
        overlap_kernel,
        out_shape=small((8, LANES)),
        in_specs=[VMEM] * 3,
        out_specs=VMEM,
    )(atom_column, weighted, ovl_deriv)

    purified, sums = pl.pallas_call(
        purify_kernel,
        out_shape=(
            jax.ShapeDtypeStruct((2, ROWS, ROWS), jnp.bfloat16),
            small((8, LANES)),
        ),
        in_specs=[SMEM] + [VMEM] * (2 * PIECES) + [HBM] * 3 + [VMEM] * 2,
        out_specs=(VMEM, VMEM),
        scratch_shapes=[
            pltpu.VMEM((2, SLABS * ROWS, ROWS), jnp.bfloat16),
            pltpu.SemaphoreType.DMA((2, SLABS)),
            pltpu.VMEM((ROWS, ROWS), jnp.float32),
            pltpu.VMEM((2, ROWS, ROWS), jnp.bfloat16),
            pltpu.VMEM((3, ROWS, ROWS), jnp.bfloat16),
            pltpu.SemaphoreType.DMA((2,)),
        ],
        compiler_params=PARAMS,
        cost_estimate=COST,
    )(
        facts,
        *wide_zero,
        *wide_one,
        tall,
        density,
        ham_deriv,
        atom_column,
        overlap,
    )

    for swap in (x_swap(1), x_swap(2), y_swap(1)):
        sums = sums + send(sums, swap)
    mass_row = masses[None, :]
    forces, sums, norms = pl.pallas_call(
        norm_kernel,
        out_shape=(small(positions.shape), small((8, LANES)), small((8, LANES))),
        in_specs=[VMEM] * 4,
        out_specs=(VMEM, VMEM, VMEM),
    )(sums, send(sums, y_swap(2)), velocities, mass_row)
    for swap in (core_swap(), z_swap(1), z_swap(2)):
        norms = norms + send(norms, swap)
    new_velocities, new_positions = pl.pallas_call(
        update_kernel,
        out_shape=(small(positions.shape), small(positions.shape)),
        in_specs=[VMEM] * 6,
        out_specs=(VMEM, VMEM),
    )(norms, send(norms, z_swap(4)), sums, positions, velocities, mass_row)
    return (purified, forces, new_velocities, new_positions)


def solution(mesh):
    in_specs = (
        P(None, "row", "col"),
        P("row", "col"),
        P(None, "row", "col"),
        P(None, "row", "col"),
        P("row", "col"),
        P(),
        P("row", None),
        P(None, "row"),
        P(None, "row"),
        P("row"),
    )
    out_specs = (P(None, "row", "col"), P(None, "row"), P(None, "row"), P(None, "row"))
    return jax.shard_map(local, mesh=mesh, in_specs=in_specs, out_specs=out_specs, check_vma=False)
```

```python
import jax
import jax.numpy as jnp
from jax import lax
from jax.experimental import pallas as pl
from jax.experimental.pallas import tpu as pltpu
from jax.sharding import PartitionSpec as P

TILE = 128
ROWS = 384
SLABS = 16
LANES = 128

mixing = 0.25
time_step = 0.1
epsilon = 1e-06

AXES = ("row", "col")


def place(z, core, x, y):
    return (z % 8 * 2 + core) * 16 + x % 4 * 4 + y % 4


def pairs(move):
    out = []
    for z in range(8):
        for core in range(2):
            for x in range(4):
                for y in range(4):
                    out.append((place(z, core, x, y), place(*move(z, core, x, y))))
    return out


def x_by(k):
    return pairs(lambda z, core, x, y: (z, core, x + k, y))


def y_by(k):
    return pairs(lambda z, core, x, y: (z, core, x, y + k))


def send(value, table):
    return lax.ppermute(value, AXES, table)


def gather_plane(block, first, second):
    one = send(block, first(1))
    two = send(block, first(-1))
    three = send(block, first(2))
    line = jnp.stack([block, one, two, three])
    ahead = send(line, second(1))
    behind = send(line, second(-1))
    far_low = send(ahead[:2], second(1))
    far_high = send(behind[2:], second(-1))
    return (line, ahead, behind, far_low, far_high)


def slots(first_at, second_at):
    order = [(a, b) for b in (0, -1, 1, 2) for a in (0, -1, 1, 2)]
    return [((first_at + a) & 3, (second_at + b) & 3) for a, b in order]


def terms_of(matrix, deriv_ref, one_hot):
    rows = []
    for x in range(3):
        column = jnp.sum(matrix * deriv_ref[x].astype(jnp.float32), axis=1, keepdims=True)
        rows.append(jnp.sum(column * one_hot, axis=0, keepdims=True))
    return rows


def one_hot_of(atom_ref):
    lanes = lax.broadcasted_iota(jnp.int32, (ROWS, LANES), 1)
    return (atom_ref[...] == lanes).astype(jnp.float32)


def overlap_kernel(atom_ref, weighted_ref, ovl_ref, out_ref):
    rows = terms_of(weighted_ref[...].astype(jnp.float32), ovl_ref, one_hot_of(atom_ref))
    out_ref[...] = jnp.zeros_like(out_ref)
    for x in range(3):
        out_ref[x : x + 1, :] = 2.0 * rows[x]


PIECES = 5
GROUPS = 4


def b_copies(facts_ref, tall_ref, b_buf, sems):
    copies = []
    for spin in range(2):
        for t in range(SLABS):
            start = pl.multiple_of(facts_ref[spin * SLABS + t] * ROWS, ROWS)
            copies.append(
                pltpu.make_async_copy(
                    tall_ref.at[spin, pl.ds(start, ROWS), :],
                    b_buf.at[spin, pl.ds(t * ROWS, ROWS), :],
                    sems.at[spin, t],
                )
            )
    return copies


def purify_kernel(facts_ref, *rest):
    wide = (rest[:PIECES], rest[PIECES : 2 * PIECES])
    tall_ref, density_ref, deriv_ref, atom_ref, overlap_ref = rest[2 * PIECES : 2 * PIECES + 5]
    out_ref, sums_ref, b_buf, sems, total, own_ref, ham_ref, own_sems = rest[2 * PIECES + 5 :]
    copies = b_copies(facts_ref, tall_ref, b_buf, sems)
    own_copy = pltpu.make_async_copy(density_ref, own_ref, own_sems.at[0])
    ham_copy = pltpu.make_async_copy(deriv_ref, ham_ref, own_sems.at[1])
    for copy in copies[:SLABS]:
        copy.start()
    own_copy.start()
    for copy in copies[SLABS:]:
        copy.start()
    ham_copy.start()
    each = SLABS // GROUPS
    for spin in range(2):
        for group in range(GROUPS):
            for copy in copies[spin * SLABS + group * each : spin * SLABS + (group + 1) * each]:
                copy.wait()
            if group < 3:
                slabs = [wide[spin][group][i] for i in range(4)]
            else:
                slabs = [wide[spin][3][0], wide[spin][3][1], wide[spin][4][0], wide[spin][4][1]]
            product = jnp.dot(
                jnp.concatenate(slabs, axis=1),
                b_buf[spin, pl.ds(group * each * ROWS, each * ROWS), :],
                preferred_element_type=jnp.float32,
            )
            if group == 0:
                total[...] = product
            else:
                total[...] += product
        square = total[...]
        if spin == 0:
            own_copy.wait()
        flip = facts_ref[2 * SLABS + spin] == 1
        raw = jnp.where(flip, 2.0 * own_ref[spin].astype(jnp.float32) - square, square)
        for i in range(3):
            for j in range(3):
                weight = facts_ref[2 * SLABS + 2 + 3 * i + j].astype(jnp.float32)
                at = (slice(i * TILE, (i + 1) * TILE), slice(j * TILE, (j + 1) * TILE))
                out_ref[(spin,) + at] = (raw[at] * weight).astype(jnp.bfloat16)
    both = out_ref[0].astype(jnp.float32) + out_ref[1].astype(jnp.float32)
    ham_copy.wait()
    rows = terms_of(both, ham_ref, one_hot_of(atom_ref))
    terms = overlap_ref[...]
    lines = lax.broadcasted_iota(jnp.int32, (8, LANES), 0)
    for x in range(3):
        terms = jnp.where(lines == x, terms - 2.0 * rows[x], terms)
    for part in range(SLABS):
        sums_ref[part] = terms


def norm_kernel(parts_ref, velocities_ref, masses_ref, forces_ref, sums_ref, norms_ref):
    sums = parts_ref[0]
    for part in range(1, parts_ref.shape[0]):
        sums = sums + parts_ref[part]
    forces = sums[:3, : forces_ref.shape[1]]
    forces_ref[...] = forces
    sums_ref[...] = sums
    scaled = forces / jnp.sqrt(masses_ref[...])
    speeds = velocities_ref[...]
    rows = lax.broadcasted_iota(jnp.int32, norms_ref.shape, 1)
    norms_ref[...] = jnp.where(rows == 0, jnp.sum(scaled * scaled), jnp.sum(speeds * speeds))


def update_kernel(
    parts_ref, sums_ref, positions_ref, velocities_ref, masses_ref, speeds_ref, places_ref
):
    norms = parts_ref[0]
    for part in range(1, parts_ref.shape[0]):
        norms = norms + parts_ref[part]
    force_norm, speed_norm = norms[0:1, 0:1], norms[1:2, 0:1]
    root_mass = jnp.sqrt(masses_ref[...])
    scaled = sums_ref[:3, : speeds_ref.shape[1]] / root_mass
    speeds = (
        (1.0 - mixing) * velocities_ref[...]
        + mixing * jnp.sqrt(speed_norm) * scaled / jnp.sqrt(force_norm + epsilon)
        + time_step * scaled
    )
    speeds_ref[...] = speeds
    places_ref[...] = positions_ref[...] + time_step * speeds / root_mass


SMEM = pl.BlockSpec(memory_space=pltpu.SMEM)
VMEM = pl.BlockSpec(memory_space=pltpu.VMEM)
HBM = pl.BlockSpec(memory_space=pltpu.HBM)

COST = pl.CostEstimate(
    flops=4 * ROWS * ROWS * ROWS * SLABS,
    bytes_accessed=8 * ROWS * ROWS * SLABS,
    transcendentals=0,
)
PARAMS = pltpu.CompilerParams(vmem_limit_bytes=45 * 1024 * 1024)


LITTLE = pltpu.CompilerParams(vmem_limit_bytes=2 * 1024 * 1024)


def small(shape):
    return jax.ShapeDtypeStruct(shape, jnp.float32)


def local(
    density,
    weighted,
    ham_deriv,
    ovl_deriv,
    tile_pattern,
    branch,
    orbital_atom,
    positions,
    velocities,
    masses,
):
    column = lax.axis_index("col")
    at_x, at_y = column >> 2, column & 3
    slabs = jnp.stack(
        [
            jnp.stack([a + b * 4 for a, b in slots(at_y, at_x)]),
            jnp.stack([a * 4 + b for a, b in slots(at_x, at_y)]),
        ]
    ).astype(jnp.int32)
    facts = jnp.concatenate([slabs.reshape(-1), branch, tile_pattern.reshape(-1)])

    tall = lax.all_gather(density, "row", axis=1, tiled=True)
    low, high = lax.optimization_barrier((density[0], density[1]))
    wide_zero = gather_plane(low, y_by, x_by)
    wide_one = gather_plane(high, x_by, y_by)

    atom_column = orbital_atom.reshape(ROWS, 1)
    overlap = pl.pallas_call(
        overlap_kernel,
        out_shape=small((8, LANES)),
        in_specs=[VMEM] * 3,
        out_specs=VMEM,
        compiler_params=pltpu.CompilerParams(vmem_limit_bytes=4 * 1024 * 1024),
    )(atom_column, weighted, ovl_deriv)

    purified, sums = pl.pallas_call(
        purify_kernel,
        out_shape=(
            jax.ShapeDtypeStruct((2, ROWS, ROWS), jnp.bfloat16),
            small((SLABS, 8, LANES)),
        ),
        in_specs=[SMEM] + [VMEM] * (2 * PIECES) + [HBM] * 3 + [VMEM] * 2,
        out_specs=(VMEM, VMEM),
        scratch_shapes=[
            pltpu.VMEM((2, SLABS * ROWS, ROWS), jnp.bfloat16),
            pltpu.SemaphoreType.DMA((2, SLABS)),
            pltpu.VMEM((ROWS, ROWS), jnp.float32),
            pltpu.VMEM((2, ROWS, ROWS), jnp.bfloat16),
            pltpu.VMEM((3, ROWS, ROWS), jnp.bfloat16),
            pltpu.SemaphoreType.DMA((2,)),
        ],
        compiler_params=PARAMS,
        cost_estimate=COST,
    )(
        facts,
        *wide_zero,
        *wide_one,
        tall,
        density,
        ham_deriv,
        atom_column,
        overlap,
    )

    parts = lax.all_to_all(sums, "col", 0, 0)
    mass_row = masses[None, :]
    forces, sums, norms = pl.pallas_call(
        norm_kernel,
        out_shape=(small(positions.shape), small((8, LANES)), small((SLABS, 8, LANES))),
        in_specs=[VMEM] * 3,
        out_specs=(VMEM, VMEM, VMEM),
        compiler_params=LITTLE,
    )(parts, velocities, mass_row)
    parts = lax.all_to_all(norms, "row", 0, 0)
    new_velocities, new_positions = pl.pallas_call(
        update_kernel,
        out_shape=(small(positions.shape), small(positions.shape)),
        in_specs=[VMEM] * 5,
        out_specs=(VMEM, VMEM),
        compiler_params=LITTLE,
    )(parts, sums, positions, velocities, mass_row)
    return (purified, forces, new_velocities, new_positions)


def solution(mesh):
    in_specs = (
        P(None, "row", "col"),
        P("row", "col"),
        P(None, "row", "col"),
        P(None, "row", "col"),
        P("row", "col"),
        P(),
        P("row", None),
        P(None, "row"),
        P(None, "row"),
        P("row"),
    )
    out_specs = (P(None, "row", "col"), P(None, "row"), P(None, "row"), P(None, "row"))
    return jax.shard_map(local, mesh=mesh, in_specs=in_specs, out_specs=out_specs, check_vma=False)
```

```python
import jax
import jax.numpy as jnp
from jax import lax
from jax.experimental import pallas as pl
from jax.experimental.pallas import tpu as pltpu
from jax.sharding import PartitionSpec as P

TILE = 128
ROWS = 384
SLABS = 16
HALVES = 2
LANES = 128

mixing = 0.25
time_step = 0.1
epsilon = 1e-06

AXES = ("row", "col")


def place(z, core, x, y):
    return (z % 8 * 2 + core) * 16 + x % 4 * 4 + y % 4


def pairs(move):
    out = []
    for z in range(8):
        for core in range(2):
            for x in range(4):
                for y in range(4):
                    out.append((place(z, core, x, y), place(*move(z, core, x, y))))
    return out


def first_by(k):
    return pairs(lambda z, core, x, y: (z, core, x + k * core, y + k * (1 - core)))


def second_by(k):
    return pairs(lambda z, core, x, y: (z, core, x + k * (1 - core), y + k * core))


def z_by(k):
    return pairs(lambda z, core, x, y: (z + k, core, x, y))


def core_swap():
    return pairs(lambda z, core, x, y: (z, 1 - core, x, y))


def send(value, table):
    return lax.ppermute(value, AXES, table)


def gather_plane(block):
    back = send(block, first_by(1))
    fore = send(block, first_by(-1))
    line = jnp.stack([block, back, fore])
    far = jnp.stack([send(back[0], first_by(1)), send(fore[1], first_by(-1))])
    line_back = send(line, second_by(1))
    line_fore = send(line, second_by(-1))
    far_back = send(far, second_by(1))
    far_fore = send(far, second_by(-1))
    line_low = send(line_back[:, 0], second_by(1))
    line_high = send(line_fore[:, 1], second_by(-1))
    far_low = send(far_back[0], second_by(1))
    far_high = send(far_fore[1], second_by(-1))
    return (
        line,
        far,
        line_back,
        far_back,
        line_fore,
        far_fore,
        line_low,
        line_high,
        far_low,
        far_high,
    )


def rank(difference):
    return jnp.where(difference == 0, 0, jnp.where(difference == 3, 1, jnp.where(difference == 1, 2, 3)))


def gather_column(block):
    back = send(block, z_by(1))
    fore = send(block, z_by(-1))
    back_two = send(back, z_by(1))
    fore_two = send(fore, z_by(-1))
    back_three = send(back_two, z_by(1))
    fore_three = send(fore_two, z_by(-1))
    low = send(back_three[0], z_by(1))
    high = send(fore_three[1], z_by(-1))
    return (block, back, back_two, back_three, fore_three, fore_two, fore, low, high)


LEVELS = (0, -1, -2, -3, 3, 2, 1)


def terms_of(matrix, deriv_ref, one_hot):
    rows = []
    for x in range(3):
        column = jnp.sum(matrix * deriv_ref[x].astype(jnp.float32), axis=1, keepdims=True)
        rows.append(jnp.sum(column * one_hot, axis=0, keepdims=True))
    return rows


def one_hot_of(atom_ref):
    lanes = lax.broadcasted_iota(jnp.int32, (ROWS, LANES), 1)
    return (atom_ref[...] == lanes).astype(jnp.float32)


def by_line(rows, scale):
    lines = lax.broadcasted_iota(jnp.int32, (8, LANES), 0)
    out = jnp.zeros((8, LANES), jnp.float32)
    for x in range(3):
        out = jnp.where(lines == x, scale * rows[x], out)
    return out


def overlap_kernel(atom_ref, weighted_ref, ovl_ref, out_ref):
    rows = terms_of(weighted_ref[...].astype(jnp.float32), ovl_ref, one_hot_of(atom_ref))
    out_ref[...] = by_line(rows, 2.0)


FACT_CORE = SLABS
FACT_BRANCH = SLABS + 1
FACT_PATTERN = SLABS + 2
FACT_Z = SLABS + 20


def purify_kernel(facts_ref, *rest):
    wide, tall, rest = rest[:10], rest[10:19], rest[19:]
    atom_ref, other_atom_ref, ham_ref, other_ham_ref, overlap_ref = rest[:5]
    keep_ref, give_ref, sums_ref, give_sums_ref, b_buf, total, done = rest[5:]
    line, far, line_back, far_back, line_fore, far_fore, line_low, line_high, far_low, far_high = wide
    core, z = facts_ref[FACT_CORE], facts_ref[FACT_Z]
    for half in range(HALVES):
        for level, offset in enumerate(LEVELS):
            slab = ((z + offset) & 7) * 2 + half
            b_buf[facts_ref[slab]] = tall[level][half]
        slab = ((z + 4) & 7) * 2 + half
        b_buf[facts_ref[slab]] = tall[7 + half][...]
    for half in range(HALVES):
        groups = [
            [line[0, half], line[1, half], line[2, half], far[half]],
            [line_back[0, half], line_back[1, half], line_back[2, half], far_back[half]],
            [line_fore[0, half], line_fore[1, half], line_fore[2, half], far_fore[half]],
        ]
        last, corner = ((line_low, far_low), (line_high, far_high))[half]
        groups.append([last[0], last[1], last[2], corner[...]])
        for i, group in enumerate(groups):
            product = jnp.dot(
                jnp.concatenate(group, axis=1),
                b_buf[4 * i : 4 * i + 4].reshape(4 * ROWS, ROWS),
                preferred_element_type=jnp.float32,
            )
            if i == 0:
                total[...] = product
            else:
                total[...] += product
        square = total[...]
        flip = facts_ref[FACT_BRANCH] == 1
        raw = jnp.where(flip, 2.0 * line[0, half].astype(jnp.float32) - square, square)
        for i in range(3):
            for j in range(3):
                weight = facts_ref[FACT_PATTERN + 9 * half + 3 * i + j].astype(jnp.float32)
                at = (slice(i * TILE, (i + 1) * TILE), slice(j * TILE, (j + 1) * TILE))
                done[(half,) + at] = (raw[at] * weight).astype(jnp.bfloat16)
    mine = done[core]
    keep_ref[...] = mine
    rows = terms_of(mine.astype(jnp.float32), ham_ref, one_hot_of(atom_ref))
    sums_ref[...] = overlap_ref[...] + by_line(rows, -2.0)
    theirs = done[1 - core]
    give_ref[...] = theirs
    rows = terms_of(theirs.astype(jnp.float32), other_ham_ref, one_hot_of(other_atom_ref))
    give_sums_ref[...] = by_line(rows, -2.0)


def norm_kernel(parts_ref, velocities_ref, masses_ref, forces_ref, sums_ref, norms_ref):
    sums = parts_ref[0]
    for part in range(1, parts_ref.shape[0]):
        sums = sums + parts_ref[part]
    forces = sums[:3, : forces_ref.shape[1]]
    forces_ref[...] = forces
    sums_ref[...] = sums
    scaled = forces / jnp.sqrt(masses_ref[...])
    speeds = velocities_ref[...]
    rows = lax.broadcasted_iota(jnp.int32, norms_ref.shape, 1)
    norms_ref[...] = jnp.where(rows == 0, jnp.sum(scaled * scaled), jnp.sum(speeds * speeds))


def update_kernel(
    parts_ref, sums_ref, positions_ref, velocities_ref, masses_ref, speeds_ref, places_ref
):
    norms = parts_ref[0]
    for part in range(1, parts_ref.shape[0]):
        norms = norms + parts_ref[part]
    force_norm, speed_norm = norms[0:1, 0:1], norms[1:2, 0:1]
    root_mass = jnp.sqrt(masses_ref[...])
    scaled = sums_ref[:3, : speeds_ref.shape[1]] / root_mass
    speeds = (
        (1.0 - mixing) * velocities_ref[...]
        + mixing * jnp.sqrt(speed_norm) * scaled / jnp.sqrt(force_norm + epsilon)
        + time_step * scaled
    )
    speeds_ref[...] = speeds
    places_ref[...] = positions_ref[...] + time_step * speeds / root_mass


SMEM = pl.BlockSpec(memory_space=pltpu.SMEM)
VMEM = pl.BlockSpec(memory_space=pltpu.VMEM)

COST = pl.CostEstimate(
    flops=4 * ROWS * ROWS * ROWS * SLABS,
    bytes_accessed=8 * ROWS * ROWS * SLABS,
    transcendentals=0,
)
PARAMS = pltpu.CompilerParams(vmem_limit_bytes=16 * 1024 * 1024)
LITTLE = pltpu.CompilerParams(vmem_limit_bytes=2 * 1024 * 1024)


def small(shape):
    return jax.ShapeDtypeStruct(shape, jnp.float32)


def half_block():
    return jax.ShapeDtypeStruct((ROWS, ROWS), jnp.bfloat16)


def local(
    density,
    weighted,
    ham_deriv,
    ovl_deriv,
    tile_pattern,
    branch,
    orbital_atom,
    positions,
    velocities,
    masses,
):
    row, column = lax.axis_index("row"), lax.axis_index("col")
    z, core = row >> 1, row & 1
    on_zero = core == 0
    at_x, at_y = column >> 2, column & 3

    mine = jnp.where(on_zero, density[0], density[1])
    theirs = send(jnp.where(on_zero, density[1], density[0]), core_swap())
    block = jnp.stack([jnp.where(on_zero, mine, theirs), jnp.where(on_zero, theirs, mine)])
    wide = gather_plane(block)
    tall = gather_column(block)

    other_ham = send(ham_deriv, core_swap())
    notes = jnp.concatenate(
        [orbital_atom.reshape(-1), tile_pattern.reshape(-1), jnp.zeros((119,), jnp.int32)]
    ).astype(jnp.float32)
    other_notes = send(notes.reshape(4, LANES), core_swap()).reshape(-1).astype(jnp.int32)
    other_atom, other_pattern = other_notes[:ROWS], other_notes[ROWS : ROWS + 9]
    own_pattern = tile_pattern.reshape(-1)

    slab = jnp.arange(SLABS, dtype=jnp.int32)
    by_x, by_y = ((slab >> 2) - at_x) & 3, ((slab & 3) - at_y) & 3
    first, second = jnp.where(on_zero, by_y, by_x), jnp.where(on_zero, by_x, by_y)
    facts = jnp.concatenate(
        [
            rank(second) * 4 + rank(first),
            jnp.stack([core, jnp.where(on_zero, branch[0], branch[1])]),
            jnp.where(on_zero, own_pattern, other_pattern),
            jnp.where(on_zero, other_pattern, own_pattern),
            jnp.stack([z]),
        ]
    ).astype(jnp.int32)

    atom_column = orbital_atom.reshape(ROWS, 1)
    overlap = pl.pallas_call(
        overlap_kernel,
        out_shape=small((8, LANES)),
        in_specs=[VMEM] * 3,
        out_specs=VMEM,
        compiler_params=pltpu.CompilerParams(vmem_limit_bytes=4 * 1024 * 1024),
    )(atom_column, weighted, ovl_deriv)

    keep, give, sums, give_sums = pl.pallas_call(
        purify_kernel,
        out_shape=(half_block(), half_block(), small((8, LANES)), small((8, LANES))),
        in_specs=[SMEM] + [VMEM] * 24,
        out_specs=(VMEM,) * 4,
        scratch_shapes=[
            pltpu.VMEM((SLABS, ROWS, ROWS), jnp.bfloat16),
            pltpu.VMEM((ROWS, ROWS), jnp.float32),
            pltpu.VMEM((HALVES, ROWS, ROWS), jnp.bfloat16),
        ],
        compiler_params=PARAMS,
        cost_estimate=COST,
    )(
        facts,
        *wide,
        *tall,
        atom_column,
        other_atom.reshape(ROWS, 1),
        ham_deriv,
        other_ham,
        overlap,
    )

    sums = sums + send(give_sums, core_swap())
    got = send(give, core_swap())
    parts = lax.all_to_all(jnp.broadcast_to(sums, (SLABS, 8, LANES)), "col", 0, 0)
    mass_row = masses[None, :]
    forces, sums, norms = pl.pallas_call(
        norm_kernel,
        out_shape=(small(positions.shape), small((8, LANES)), small((SLABS, 8, LANES))),
        in_specs=[VMEM] * 3,
        out_specs=(VMEM, VMEM, VMEM),
        compiler_params=LITTLE,
    )(parts, velocities, mass_row)
    parts = lax.all_to_all(norms, "row", 0, 0)
    new_velocities, new_positions = pl.pallas_call(
        update_kernel,
        out_shape=(small(positions.shape), small(positions.shape)),
        in_specs=[VMEM] * 5,
        out_specs=(VMEM, VMEM),
        compiler_params=LITTLE,
    )(parts, sums, positions, velocities, mass_row)
    purified = jnp.stack([jnp.where(on_zero, keep, got), jnp.where(on_zero, got, keep)])
    return (purified, forces, new_velocities, new_positions)


def solution(mesh):
    in_specs = (
        P(None, "row", "col"),
        P("row", "col"),
        P(None, "row", "col"),
        P(None, "row", "col"),
        P("row", "col"),
        P(),
        P("row", None),
        P(None, "row"),
        P(None, "row"),
        P("row"),
    )
    out_specs = (P(None, "row", "col"), P(None, "row"), P(None, "row"), P(None, "row"))
    return jax.shard_map(local, mesh=mesh, in_specs=in_specs, out_specs=out_specs, check_vma=False)
```

```python
import jax
import jax.numpy as jnp
from jax import lax
from jax.experimental import pallas as pl
from jax.experimental.pallas import tpu as pltpu
from jax.sharding import PartitionSpec as P

TILE = 128
ROWS = 384
SLABS = 16
HALVES = 2
LANES = 128

mixing = 0.25
time_step = 0.1
epsilon = 1e-06

AXES = ("row", "col")


def place(z, core, x, y):
    return (z % 8 * 2 + core) * 16 + x % 4 * 4 + y % 4


def pairs(move):
    out = []
    for z in range(8):
        for core in range(2):
            for x in range(4):
                for y in range(4):
                    out.append((place(z, core, x, y), place(*move(z, core, x, y))))
    return out


def first_by(k):
    return pairs(lambda z, core, x, y: (z, core, x + k * core, y + k * (1 - core)))


def second_by(k):
    return pairs(lambda z, core, x, y: (z, core, x + k * (1 - core), y + k * core))


def z_by(k):
    return pairs(lambda z, core, x, y: (z + k, core, x, y))


def core_swap():
    return pairs(lambda z, core, x, y: (z, 1 - core, x, y))


def send(value, table):
    return lax.ppermute(value, AXES, table)


def after(value, *others):
    return lax.optimization_barrier((value,) + others)[0]


def gather(block):
    z_back = send(block, z_by(1))
    z_fore = send(block, z_by(-1))
    back = send(block, first_by(1))
    fore = send(block, first_by(-1))
    far = send(block, first_by(2))
    back, fore, far = after((back, fore, far), z_back, z_fore)
    line = jnp.stack([block, back, fore, far])
    line_back = send(line, second_by(1))
    line_fore = send(line, second_by(-1))
    z_back_two = send(z_back, z_by(1))
    z_fore_two = send(z_fore, z_by(-1))
    z_back_three = send(z_back_two, z_by(1))
    z_fore_three = send(z_fore_two, z_by(-1))
    low, high = after((line_back[:, 0], line_fore[:, 1]), z_back_three, z_fore_three)
    line_low = send(low, second_by(1))
    line_high = send(high, second_by(-1))
    z_low = send(z_back_three[0], z_by(1))
    z_high = send(z_fore_three[1], z_by(-1))
    wide = (line, line_back, line_fore, line_low, line_high)
    tall = (
        block,
        z_back,
        z_back_two,
        z_back_three,
        z_fore_three,
        z_fore_two,
        z_fore,
        z_low,
        z_high,
    )
    return wide, tall


LEVELS = (0, -1, -2, -3, 3, 2, 1)


def position():
    row, column = lax.axis_index("row"), lax.axis_index("col")
    return row >> 1, row & 1, column >> 2, column & 3


def terms_of(matrix, deriv_ref, one_hot):
    rows = []
    for x in range(3):
        column = jnp.sum(matrix * deriv_ref[x].astype(jnp.float32), axis=1, keepdims=True)
        rows.append(jnp.sum(column * one_hot, axis=0, keepdims=True))
    return rows


def one_hot_of(atom_ref):
    atoms = jnp.broadcast_to(atom_ref[...].astype(jnp.float32), (LANES, ROWS))
    lanes = lax.broadcasted_iota(jnp.int32, (ROWS, LANES), 1).astype(jnp.float32)
    return (jnp.transpose(atoms) == lanes).astype(jnp.float32)


def by_line(rows, scale):
    lines = lax.broadcasted_iota(jnp.int32, (8, LANES), 0)
    out = jnp.zeros((8, LANES), jnp.float32)
    for x in range(3):
        out = jnp.where(lines == x, scale * rows[x], out)
    return out


def overlap_kernel(atom_ref, weighted_ref, ovl_ref, out_ref):
    rows = terms_of(weighted_ref[...].astype(jnp.float32), ovl_ref, one_hot_of(atom_ref))
    out_ref[...] = by_line(rows, 2.0)


def give_kernel(density_ref, give_ref, sem):
    core = position()[1]
    copy = pltpu.make_async_copy(density_ref.at[1 - core], give_ref, sem)
    copy.start()
    copy.wait()


def block_kernel(density_ref, got_ref, block_ref, sems):
    core = position()[1]
    mine = pltpu.make_async_copy(density_ref.at[core], block_ref.at[core], sems.at[0])
    theirs = pltpu.make_async_copy(got_ref, block_ref.at[1 - core], sems.at[1])
    mine.start()
    theirs.start()
    mine.wait()
    theirs.wait()


def purify_kernel(branch_ref, pattern_ref, other_pattern_ref, *rest):
    wide, tall, rest = rest[:5], rest[5:14], rest[14:]
    ham_ref, other_ham_ref, atom_ref, other_atom_ref, overlap_ref = rest[:5]
    out_ref, give_ref, sums_ref, b_buf, total, done, out_sem = rest[5:]
    line = wide[0]
    z, core, at_x, at_y = position()
    for half in range(HALVES):
        for level, offset in enumerate(LEVELS + (4,)):
            slab = ((z + offset) & 7) * 2 + half
            by_x, by_y = ((slab >> 2) - at_x) & 3, ((slab & 3) - at_y) & 3
            first = jnp.where(core == 0, by_y, by_x)
            second = jnp.where(core == 0, by_x, by_y)
            first = jnp.where(first == 3, 1, first + jnp.minimum(first, 1))
            second = jnp.where(second == 3, 1, second + jnp.minimum(second, 1))
            slot = second * 4 + first
            b_buf[slot] = tall[level][half] if level < 7 else tall[7 + half][...]
    for group in range(4):
        rows = b_buf[4 * group : 4 * group + 4].reshape(4 * ROWS, ROWS)
        for half in range(HALVES):
            if group < 3:
                slabs = [wide[group][i, half] for i in range(4)]
            else:
                slabs = [wide[3 + half][i] for i in range(4)]
            product = jnp.dot(
                jnp.concatenate(slabs, axis=1),
                rows,
                preferred_element_type=jnp.float32,
            )
            if group == 0:
                total[half] = product
            else:
                total[half] += product
    for half in range(HALVES):
        square = total[half]
        flip = branch_ref[core] == 1
        raw = jnp.where(flip, 2.0 * line[0, half].astype(jnp.float32) - square, square)
        for i in range(3):
            for j in range(3):
                weight = jnp.where(core == half, pattern_ref[i, j], other_pattern_ref[i, j])
                at = (slice(i * TILE, (i + 1) * TILE), slice(j * TILE, (j + 1) * TILE))
                done[(half,) + at] = (raw[at] * weight.astype(jnp.float32)).astype(jnp.bfloat16)
    out_copy = pltpu.make_async_copy(done.at[core], out_ref.at[core], out_sem)
    out_copy.start()
    mine = terms_of(done[core].astype(jnp.float32), ham_ref, one_hot_of(atom_ref))
    mine = overlap_ref[...] + by_line(mine, -2.0)
    theirs = done[1 - core]
    give_ref[...] = theirs
    theirs = terms_of(theirs.astype(jnp.float32), other_ham_ref, one_hot_of(other_atom_ref))
    theirs = by_line(theirs, -2.0)
    zero, one = jnp.where(core == 0, mine, theirs), jnp.where(core == 0, theirs, mine)
    for part in range(SLABS):
        sums_ref[part] = zero
        sums_ref[SLABS + part] = one
    out_copy.wait()


def norm_kernel(parts_ref, velocities_ref, masses_ref, forces_ref, sums_ref, norms_ref):
    sums = parts_ref[0]
    for part in range(1, parts_ref.shape[0]):
        sums = sums + parts_ref[part]
    forces = sums[:3, : forces_ref.shape[1]]
    forces_ref[...] = forces
    sums_ref[...] = sums
    scaled = forces / jnp.sqrt(masses_ref[...])
    speeds = velocities_ref[...]
    rows = lax.broadcasted_iota(jnp.int32, norms_ref.shape, 1)
    norms_ref[...] = jnp.where(rows == 0, jnp.sum(scaled * scaled), jnp.sum(speeds * speeds))


def update_kernel(
    got_ref,
    half_ref,
    parts_ref,
    sums_ref,
    positions_ref,
    velocities_ref,
    masses_ref,
    out_ref,
    speeds_ref,
    places_ref,
    out_sem,
):
    del half_ref
    out_copy = pltpu.make_async_copy(got_ref, out_ref.at[1 - position()[1]], out_sem)
    out_copy.start()
    norms = parts_ref[0]
    for part in range(1, parts_ref.shape[0]):
        norms = norms + parts_ref[part]
    force_norm, speed_norm = norms[0:1, 0:1], norms[1:2, 0:1]
    root_mass = jnp.sqrt(masses_ref[...])
    scaled = sums_ref[:3, : speeds_ref.shape[1]] / root_mass
    speeds = (
        (1.0 - mixing) * velocities_ref[...]
        + mixing * jnp.sqrt(speed_norm) * scaled / jnp.sqrt(force_norm + epsilon)
        + time_step * scaled
    )
    speeds_ref[...] = speeds
    places_ref[...] = positions_ref[...] + time_step * speeds / root_mass
    out_copy.wait()


SMEM = pl.BlockSpec(memory_space=pltpu.SMEM)
VMEM = pl.BlockSpec(memory_space=pltpu.VMEM)
HBM = pl.BlockSpec(memory_space=pltpu.HBM)

COST = pl.CostEstimate(
    flops=4 * ROWS * ROWS * ROWS * SLABS,
    bytes_accessed=8 * ROWS * ROWS * SLABS,
    transcendentals=0,
)
PARAMS = pltpu.CompilerParams(vmem_limit_bytes=28 * 1024 * 1024)
LITTLE = pltpu.CompilerParams(vmem_limit_bytes=2 * 1024 * 1024)


def small(shape):
    return jax.ShapeDtypeStruct(shape, jnp.float32)


def local(
    density,
    weighted,
    ham_deriv,
    ovl_deriv,
    tile_pattern,
    branch,
    orbital_atom,
    positions,
    velocities,
    masses,
):
    block_type = jax.ShapeDtypeStruct((ROWS, ROWS), jnp.bfloat16)
    give = pl.pallas_call(
        give_kernel,
        out_shape=block_type,
        in_specs=[HBM],
        out_specs=VMEM,
        scratch_shapes=[pltpu.SemaphoreType.DMA],
        compiler_params=LITTLE,
    )(density)
    block = pl.pallas_call(
        block_kernel,
        out_shape=jax.ShapeDtypeStruct((HALVES, ROWS, ROWS), jnp.bfloat16),
        in_specs=[HBM, VMEM],
        out_specs=VMEM,
        scratch_shapes=[pltpu.SemaphoreType.DMA((2,))],
        compiler_params=LITTLE,
    )(density, send(give, core_swap()))
    wide, tall = gather(block)

    other_ham = send(ham_deriv, core_swap())
    other_atom = send(orbital_atom, core_swap())
    other_pattern = send(tile_pattern, core_swap())

    overlap = pl.pallas_call(
        overlap_kernel,
        out_shape=small((8, LANES)),
        in_specs=[VMEM] * 3,
        out_specs=VMEM,
        compiler_params=pltpu.CompilerParams(vmem_limit_bytes=4 * 1024 * 1024),
    )(orbital_atom, weighted, ovl_deriv)

    half, give, sums = pl.pallas_call(
        purify_kernel,
        out_shape=(
            jax.ShapeDtypeStruct((2, ROWS, ROWS), jnp.bfloat16),
            block_type,
            small((2 * SLABS, 8, LANES)),
        ),
        in_specs=[SMEM] * 3 + [VMEM] * 19,
        out_specs=(HBM, VMEM, VMEM),
        scratch_shapes=[
            pltpu.VMEM((SLABS, ROWS, ROWS), jnp.bfloat16),
            pltpu.VMEM((HALVES, ROWS, ROWS), jnp.float32),
            pltpu.VMEM((HALVES, ROWS, ROWS), jnp.bfloat16),
            pltpu.SemaphoreType.DMA,
        ],
        compiler_params=PARAMS,
        cost_estimate=COST,
    )(
        branch,
        tile_pattern,
        other_pattern,
        *wide,
        *tall,
        ham_deriv,
        other_ham,
        orbital_atom,
        other_atom,
        overlap,
    )
    got = send(give, core_swap())

    planes = [[(2 * z + c) * SLABS + i for c in range(2) for i in range(SLABS)] for z in range(8)]
    parts = lax.all_to_all(sums, AXES, 0, 0, axis_index_groups=planes)
    mass_row = masses[None, :]
    forces, sums, norms = pl.pallas_call(
        norm_kernel,
        out_shape=(small(positions.shape), small((8, LANES)), small((SLABS, 8, LANES))),
        in_specs=[VMEM] * 3,
        out_specs=(VMEM, VMEM, VMEM),
        compiler_params=LITTLE,
    )(parts, velocities, mass_row)
    parts = lax.all_to_all(norms, "row", 0, 0)
    purified, new_velocities, new_positions = pl.pallas_call(
        update_kernel,
        out_shape=(
            jax.ShapeDtypeStruct((2, ROWS, ROWS), jnp.bfloat16),
            small(positions.shape),
            small(positions.shape),
        ),
        in_specs=[HBM, HBM] + [VMEM] * 5,
        out_specs=(HBM, VMEM, VMEM),
        scratch_shapes=[pltpu.SemaphoreType.DMA],
        input_output_aliases={1: 0},
        compiler_params=LITTLE,
    )(got, half, parts, sums, positions, velocities, mass_row)
    return (purified, forces, new_velocities, new_positions)


def solution(mesh):
    in_specs = (
        P(None, "row", "col"),
        P("row", "col"),
        P(None, "row", "col"),
        P(None, "row", "col"),
        P("row", "col"),
        P(),
        P("row", None),
        P(None, "row"),
        P(None, "row"),
        P("row"),
    )
    out_specs = (P(None, "row", "col"), P(None, "row"), P(None, "row"), P(None, "row"))
    return jax.shard_map(local, mesh=mesh, in_specs=in_specs, out_specs=out_specs, check_vma=False)
```

```python
import jax
import jax.numpy as jnp
from jax import lax
from jax.experimental import pallas as pl
from jax.experimental.pallas import tpu as pltpu
from jax.sharding import PartitionSpec as P

TILE = 128
ROWS = 384
SLABS = 16
HALVES = 2
LANES = 128

mixing = 0.25
time_step = 0.1
epsilon = 1e-06

AXES = ("row", "col")


def place(z, core, x, y):
    return (z % 8 * 2 + core) * 16 + x % 4 * 4 + y % 4


def pairs(move):
    out = []
    for z in range(8):
        for core in range(2):
            for x in range(4):
                for y in range(4):
                    out.append((place(z, core, x, y), place(*move(z, core, x, y))))
    return out


def first_by(k):
    return pairs(lambda z, core, x, y: (z, core, x + k * core, y + k * (1 - core)))


def second_by(k):
    return pairs(lambda z, core, x, y: (z, core, x + k * (1 - core), y + k * core))


def z_by(k):
    return pairs(lambda z, core, x, y: (z + k, core, x, y))


def core_swap():
    return pairs(lambda z, core, x, y: (z, 1 - core, x, y))


def send(value, table):
    return lax.ppermute(value, AXES, table)


def after(value, *others):
    return lax.optimization_barrier((value,) + others)[0]


def gather(block):
    z_back = send(block, z_by(1))
    z_fore = send(block, z_by(-1))
    back = send(block, first_by(1))
    fore = send(block, first_by(-1))
    far = send(block, first_by(2))
    back, fore, far = after((back, fore, far), z_back, z_fore)
    line = jnp.stack([block, back, fore, far])
    line_back = send(line, second_by(1))
    line_fore = send(line, second_by(-1))
    z_back_two = send(z_back, z_by(1))
    z_fore_two = send(z_fore, z_by(-1))
    z_back_three = send(z_back_two, z_by(1))
    z_fore_three = send(z_fore_two, z_by(-1))
    low, high = after((line_back[:, 0], line_fore[:, 1]), z_back_three, z_fore_three)
    line_low = send(low, second_by(1))
    line_high = send(high, second_by(-1))
    z_low = send(z_back_three[0], z_by(1))
    z_high = send(z_fore_three[1], z_by(-1))
    wide = (line, line_back, line_fore, line_low, line_high)
    tall = (
        block,
        z_back,
        z_back_two,
        z_back_three,
        z_fore_three,
        z_fore_two,
        z_fore,
        z_low,
        z_high,
    )
    return wide, tall


LEVELS = (0, -1, -2, -3, 3, 2, 1)


def position():
    row, column = lax.axis_index("row"), lax.axis_index("col")
    return row >> 1, row & 1, column >> 2, column & 3


def terms_of(matrix, deriv_ref, one_hot):
    rows = []
    for x in range(3):
        column = jnp.sum(matrix * deriv_ref[x].astype(jnp.float32), axis=1, keepdims=True)
        rows.append(jnp.sum(column * one_hot, axis=0, keepdims=True))
    return rows


def one_hot_of(atom_ref):
    atoms = jnp.broadcast_to(atom_ref[...].astype(jnp.float32), (LANES, ROWS))
    lanes = lax.broadcasted_iota(jnp.int32, (ROWS, LANES), 1).astype(jnp.float32)
    return (jnp.transpose(atoms) == lanes).astype(jnp.float32)


def by_line(zero, one, scale):
    lines = lax.broadcasted_iota(jnp.int32, (8, LANES), 0)
    out = jnp.zeros((8, LANES), jnp.float32)
    for x in range(3):
        out = jnp.where(lines == x, scale * zero[x], out)
        out = jnp.where(lines == 3 + x, scale * one[x], out)
    return out


def overlap_kernel(atom_ref, weighted_ref, ovl_ref, out_ref):
    rows = terms_of(weighted_ref[...].astype(jnp.float32), ovl_ref, one_hot_of(atom_ref))
    lines = lax.broadcasted_iota(jnp.int32, (8, LANES), 0)
    own = (lines >= 3) == (position()[1] == 1)
    out_ref[...] = jnp.where(own, by_line(rows, rows, 2.0), 0.0)


def give_kernel(density_ref, give_ref, sem):
    core = position()[1]
    copy = pltpu.make_async_copy(density_ref.at[1 - core], give_ref, sem)
    copy.start()
    copy.wait()


def block_kernel(density_ref, got_ref, block_ref, sems):
    core = position()[1]
    mine = pltpu.make_async_copy(density_ref.at[core], block_ref.at[core], sems.at[0])
    theirs = pltpu.make_async_copy(got_ref, block_ref.at[1 - core], sems.at[1])
    mine.start()
    theirs.start()
    mine.wait()
    theirs.wait()


def slot_of(level, half):
    _, core, at_x, at_y = position()
    slab = (level & 7) * 2 + half
    by_x, by_y = ((slab >> 2) - at_x) & 3, ((slab & 3) - at_y) & 3
    first = jnp.where(core == 0, by_y, by_x)
    second = jnp.where(core == 0, by_x, by_y)
    first = jnp.where(first == 3, 1, first + jnp.minimum(first, 1))
    second = jnp.where(second == 3, 1, second + jnp.minimum(second, 1))
    return second * 4 + first


NEAR = 12


def near_kernel(*refs):
    wide, tall, (total_ref, b_far_ref, a_far_ref, b_buf) = refs[:3], refs[3:10], refs[10:]
    z = position()[0]
    for half in range(HALVES):
        for level, offset in enumerate(LEVELS):
            b_buf[slot_of(z + offset, half)] = tall[level][half]
        slot = slot_of(z + 4, half)
        b_buf[slot] = jnp.zeros((ROWS, ROWS), jnp.bfloat16)

        @pl.when(slot >= NEAR)
        def _():
            a_far_ref[half] = jnp.zeros(a_far_ref.shape[1:], jnp.bfloat16)

        for t in range(NEAR):

            @pl.when(slot == t)
            def _():
                a_far_ref[half] = wide[t // 4][t % 4]

    b_far_ref[...] = b_buf[NEAR:]
    for group in range(3):
        rows = b_buf[4 * group : 4 * group + 4].reshape(4 * ROWS, ROWS)
        for half in range(HALVES):
            product = jnp.dot(
                jnp.concatenate([wide[group][i, half] for i in range(4)], axis=1),
                rows,
                preferred_element_type=jnp.float32,
            )
            if group == 0:
                total_ref[half] = product
            else:
                total_ref[half] += product


def purify_kernel(
    branch_ref,
    pattern_ref,
    other_pattern_ref,
    block_ref,
    line_low,
    line_high,
    z_low,
    z_high,
    total_ref,
    b_far_ref,
    a_far_ref,
    ham_ref,
    other_ham_ref,
    atom_ref,
    other_atom_ref,
    overlap_ref,
    out_ref,
    give_ref,
    sums_ref,
    b_buf,
    done,
    out_sem,
):
    z, core, _, _ = position()
    b_buf[: SLABS - NEAR] = b_far_ref[...]
    for half, piece in enumerate((z_low, z_high)):
        slot = slot_of(z + 4, half)
        b_buf[SLABS - NEAR + half] = piece[...]

        @pl.when(slot >= NEAR)
        def _():
            b_buf[slot - NEAR] = piece[...]

    rows = b_buf[...].reshape((SLABS - NEAR + 2) * ROWS, ROWS)
    for half in range(HALVES):
        lead = line_low if half == 0 else line_high
        columns = [lead[i] for i in range(4)] + [a_far_ref[i, half] for i in range(2)]
        square = total_ref[half] + jnp.dot(
            jnp.concatenate(columns, axis=1), rows, preferred_element_type=jnp.float32
        )
        flip = branch_ref[core] == 1
        raw = jnp.where(flip, 2.0 * block_ref[half].astype(jnp.float32) - square, square)
        for i in range(3):
            for j in range(3):
                weight = jnp.where(core == half, pattern_ref[i, j], other_pattern_ref[i, j])
                at = (slice(i * TILE, (i + 1) * TILE), slice(j * TILE, (j + 1) * TILE))
                done[(half,) + at] = (raw[at] * weight.astype(jnp.float32)).astype(jnp.bfloat16)
    out_copy = pltpu.make_async_copy(done.at[core], out_ref.at[core], out_sem)
    out_copy.start()
    mine = terms_of(done[core].astype(jnp.float32), ham_ref, one_hot_of(atom_ref))
    theirs = done[1 - core]
    give_ref[...] = theirs
    theirs = terms_of(theirs.astype(jnp.float32), other_ham_ref, one_hot_of(other_atom_ref))
    zero = [jnp.where(core == 0, a, b) for a, b in zip(mine, theirs)]
    one = [jnp.where(core == 0, b, a) for a, b in zip(mine, theirs)]
    sums = overlap_ref[...] + by_line(zero, one, -2.0)
    for part in range(SLABS):
        sums_ref[part] = sums
    out_copy.wait()


def norm_kernel(parts_ref, velocities_ref, masses_ref, all_ref):
    sums = parts_ref[0]
    for part in range(1, parts_ref.shape[0]):
        sums = sums + parts_ref[part]
    speeds = velocities_ref[...]
    atoms = masses_ref.shape[1]
    for part in range(all_ref.shape[0]):
        all_ref[part] = sums
        all_ref[part, 6:7, :] = jnp.ones((1, LANES), jnp.float32)
        all_ref[part, 6:7, :atoms] = masses_ref[...]
        all_ref[part, 7:8, :] = jnp.broadcast_to(jnp.sum(speeds * speeds), (1, LANES))


def update_kernel(
    got_ref,
    half_ref,
    all_ref,
    positions_ref,
    velocities_ref,
    masses_ref,
    out_ref,
    forces_ref,
    speeds_ref,
    places_ref,
    out_sem,
):
    del half_ref
    z, core, _, _ = position()
    out_copy = pltpu.make_async_copy(got_ref, out_ref.at[1 - core], out_sem)
    out_copy.start()
    squares = jnp.zeros((3, LANES), jnp.float32)
    speed_norm = jnp.zeros((1, 1), jnp.float32)
    for level in range(all_ref.shape[0] // 2):
        zero, one = all_ref[2 * level], all_ref[2 * level + 1]
        both = zero + one
        for half, mass in enumerate((zero[6:7], one[6:7])):
            scaled = both[3 * half : 3 * half + 3] / jnp.sqrt(mass)
            squares = squares + scaled * scaled
        speed_norm = speed_norm + zero[7:8, 0:1] + one[7:8, 0:1]
    force_norm = jnp.sum(squares)
    both = all_ref[2 * z] + all_ref[2 * z + 1]
    forces = jnp.where(core == 0, both[0:3], both[3:6])[:, : forces_ref.shape[1]]
    forces_ref[...] = forces
    root_mass = jnp.sqrt(masses_ref[...])
    scaled = forces / root_mass
    speeds = (
        (1.0 - mixing) * velocities_ref[...]
        + mixing * jnp.sqrt(speed_norm) * scaled / jnp.sqrt(force_norm + epsilon)
        + time_step * scaled
    )
    speeds_ref[...] = speeds
    places_ref[...] = positions_ref[...] + time_step * speeds / root_mass
    out_copy.wait()


SMEM = pl.BlockSpec(memory_space=pltpu.SMEM)
VMEM = pl.BlockSpec(memory_space=pltpu.VMEM)
HBM = pl.BlockSpec(memory_space=pltpu.HBM)

def cost(slots):
    return pl.CostEstimate(
        flops=4 * ROWS * ROWS * ROWS * slots,
        bytes_accessed=8 * ROWS * ROWS * slots,
        transcendentals=0,
    )


PARAMS = pltpu.CompilerParams(vmem_limit_bytes=12 * 1024 * 1024)
LITTLE = pltpu.CompilerParams(vmem_limit_bytes=2 * 1024 * 1024)


def small(shape):
    return jax.ShapeDtypeStruct(shape, jnp.float32)


def local(
    density,
    weighted,
    ham_deriv,
    ovl_deriv,
    tile_pattern,
    branch,
    orbital_atom,
    positions,
    velocities,
    masses,
):
    give = pl.pallas_call(
        give_kernel,
        out_shape=jax.ShapeDtypeStruct((ROWS, ROWS), jnp.bfloat16),
        in_specs=[HBM],
        out_specs=VMEM,
        scratch_shapes=[pltpu.SemaphoreType.DMA],
        compiler_params=LITTLE,
    )(density)
    block = pl.pallas_call(
        block_kernel,
        out_shape=jax.ShapeDtypeStruct((HALVES, ROWS, ROWS), jnp.bfloat16),
        in_specs=[HBM, VMEM],
        out_specs=VMEM,
        scratch_shapes=[pltpu.SemaphoreType.DMA((2,))],
        compiler_params=LITTLE,
    )(density, send(give, core_swap()))
    wide, tall = gather(block)

    other_ham = send(ham_deriv, core_swap())
    other_atom = send(orbital_atom, core_swap())
    other_pattern = send(tile_pattern, core_swap())

    overlap = pl.pallas_call(
        overlap_kernel,
        out_shape=small((8, LANES)),
        in_specs=[VMEM] * 3,
        out_specs=VMEM,
        compiler_params=pltpu.CompilerParams(vmem_limit_bytes=4 * 1024 * 1024),
    )(orbital_atom, weighted, ovl_deriv)

    total, b_far, a_far = pl.pallas_call(
        near_kernel,
        out_shape=(
            small((HALVES, ROWS, ROWS)),
            jax.ShapeDtypeStruct((SLABS - NEAR, ROWS, ROWS), jnp.bfloat16),
            jax.ShapeDtypeStruct((2, HALVES, ROWS, ROWS), jnp.bfloat16),
        ),
        in_specs=[VMEM] * 10,
        out_specs=(VMEM,) * 3,
        scratch_shapes=[pltpu.VMEM((SLABS, ROWS, ROWS), jnp.bfloat16)],
        compiler_params=PARAMS,
        cost_estimate=cost(NEAR),
    )(*wide[:3], *tall[:7])
    half, give, sums = pl.pallas_call(
        purify_kernel,
        out_shape=(
            jax.ShapeDtypeStruct((2, ROWS, ROWS), jnp.bfloat16),
            jax.ShapeDtypeStruct((ROWS, ROWS), jnp.bfloat16),
            small((SLABS, 8, LANES)),
        ),
        in_specs=[SMEM] * 3 + [VMEM] * 13,
        out_specs=(HBM, VMEM, VMEM),
        scratch_shapes=[
            pltpu.VMEM((SLABS - NEAR + 2, ROWS, ROWS), jnp.bfloat16),
            pltpu.VMEM((HALVES, ROWS, ROWS), jnp.bfloat16),
            pltpu.SemaphoreType.DMA,
        ],
        compiler_params=PARAMS,
        cost_estimate=cost(SLABS - NEAR + 2),
    )(
        branch,
        tile_pattern,
        other_pattern,
        block,
        *wide[3:],
        *tall[7:],
        total,
        b_far,
        a_far,
        ham_deriv,
        other_ham,
        orbital_atom,
        other_atom,
        overlap,
    )
    got = send(give, core_swap())

    parts = lax.all_to_all(sums, "col", 0, 0)
    mass_row = masses[None, :]
    parts = pl.pallas_call(
        norm_kernel,
        out_shape=small((SLABS, 8, LANES)),
        in_specs=[VMEM] * 3,
        out_specs=VMEM,
        compiler_params=LITTLE,
    )(parts, velocities, mass_row)
    parts = lax.all_to_all(parts, "row", 0, 0)
    purified, forces, new_velocities, new_positions = pl.pallas_call(
        update_kernel,
        out_shape=(jax.ShapeDtypeStruct((2, ROWS, ROWS), jnp.bfloat16),)
        + (small(positions.shape),) * 3,
        in_specs=[HBM, HBM] + [VMEM] * 4,
        out_specs=(HBM, VMEM, VMEM, VMEM),
        scratch_shapes=[pltpu.SemaphoreType.DMA],
        input_output_aliases={1: 0},
        compiler_params=LITTLE,
    )(got, half, parts, positions, velocities, mass_row)
    return (purified, forces, new_velocities, new_positions)


def solution(mesh):
    in_specs = (
        P(None, "row", "col"),
        P("row", "col"),
        P(None, "row", "col"),
        P(None, "row", "col"),
        P("row", "col"),
        P(),
        P("row", None),
        P(None, "row"),
        P(None, "row"),
        P("row"),
    )
    out_specs = (P(None, "row", "col"), P(None, "row"), P(None, "row"), P(None, "row"))
    return jax.shard_map(local, mesh=mesh, in_specs=in_specs, out_specs=out_specs, check_vma=False)
```

```python
import jax
import jax.numpy as jnp
from jax import lax
from jax.experimental import pallas as pl
from jax.experimental.pallas import tpu as pltpu
from jax.sharding import PartitionSpec as P

TILE = 128
ROWS = 384
SLABS = 16
HALVES = 2
LANES = 128

mixing = 0.25
time_step = 0.1
epsilon = 1e-06

AXES = ("row", "col")


def place(z, core, x, y):
    return (z % 8 * 2 + core) * 16 + x % 4 * 4 + y % 4


def pairs(move):
    out = []
    for z in range(8):
        for core in range(2):
            for x in range(4):
                for y in range(4):
                    out.append((place(z, core, x, y), place(*move(z, core, x, y))))
    return out


def first_by(k):
    return pairs(lambda z, core, x, y: (z, core, x + k * core, y + k * (1 - core)))


def second_by(k):
    return pairs(lambda z, core, x, y: (z, core, x + k * (1 - core), y + k * core))


def z_by(k):
    return pairs(lambda z, core, x, y: (z + k, core, x, y))


def core_swap():
    return pairs(lambda z, core, x, y: (z, 1 - core, x, y))


def send(value, table):
    return lax.ppermute(value, AXES, table)


def after(value, *others):
    return lax.optimization_barrier((value,) + others)[0]


EARLY = 3 << 32


def gather(block):
    z_back = send(block, z_by(1))
    z_fore = send(block, z_by(-1))
    back = send(block, first_by(1))
    fore = send(block, first_by(-1))
    far = send(block, first_by(2))
    line = jnp.stack([block, back, fore, far])
    line_back = send(line, second_by(1))
    line_fore = send(line, second_by(-1))
    z_back_two = send(z_back, z_by(1))
    z_fore_two = send(z_fore, z_by(-1))
    z_back_three = send(z_back_two, z_by(1))
    z_fore_three = send(z_fore_two, z_by(-1))
    levels = (block, z_back, z_back_two, z_back_three, z_fore_three, z_fore_two, z_fore)
    columns = pl.pallas_call(
        column_kernel,
        out_shape=jax.ShapeDtypeStruct((SLABS, ROWS, ROWS), jnp.bfloat16),
        in_specs=[VMEM] * 7,
        out_specs=VMEM,
        compiler_params=LITTLE,
        cost_estimate=pl.CostEstimate(flops=EARLY, bytes_accessed=1 << 22, transcendentals=0),
    )(*levels)
    low, high = after((line_back[:, 0], line_fore[:, 1]), columns)
    line_low = send(low, second_by(1))
    line_high = send(high, second_by(-1))
    z_low = send(z_back_three[0], z_by(1))
    z_high = send(z_fore_three[1], z_by(-1))
    return (line, line_back, line_fore), (line_low, line_high), columns, (z_low, z_high)


LEVELS = (0, -1, -2, -3, 3, 2, 1)


def position():
    row, column = lax.axis_index("row"), lax.axis_index("col")
    return row >> 1, row & 1, column >> 2, column & 3


def terms_of(matrix, deriv_ref, one_hot):
    rows = []
    for x in range(3):
        column = jnp.sum(matrix * deriv_ref[x].astype(jnp.float32), axis=1, keepdims=True)
        rows.append(jnp.sum(column * one_hot, axis=0, keepdims=True))
    return rows


def one_hot_of(atom_ref):
    atoms = jnp.broadcast_to(atom_ref[...].astype(jnp.float32), (LANES, ROWS))
    lanes = lax.broadcasted_iota(jnp.int32, (ROWS, LANES), 1).astype(jnp.float32)
    return (jnp.transpose(atoms) == lanes).astype(jnp.float32)


def by_line(zero, one, scale):
    lines = lax.broadcasted_iota(jnp.int32, (8, LANES), 0)
    out = jnp.zeros((8, LANES), jnp.float32)
    for x in range(3):
        out = jnp.where(lines == x, scale * zero[x], out)
        out = jnp.where(lines == 3 + x, scale * one[x], out)
    return out


def overlap_kernel(atom_ref, weighted_ref, ovl_ref, out_ref):
    rows = terms_of(weighted_ref[...].astype(jnp.float32), ovl_ref, one_hot_of(atom_ref))
    lines = lax.broadcasted_iota(jnp.int32, (8, LANES), 0)
    own = (lines >= 3) == (position()[1] == 1)
    out_ref[...] = jnp.where(own, by_line(rows, rows, 2.0), 0.0)


def give_kernel(density_ref, give_ref, sem):
    core = position()[1]
    copy = pltpu.make_async_copy(density_ref.at[1 - core], give_ref, sem)
    copy.start()
    copy.wait()


def block_kernel(density_ref, got_ref, block_ref, sems):
    core = position()[1]
    mine = pltpu.make_async_copy(density_ref.at[core], block_ref.at[core], sems.at[0])
    theirs = pltpu.make_async_copy(got_ref, block_ref.at[1 - core], sems.at[1])
    mine.start()
    theirs.start()
    mine.wait()
    theirs.wait()


def slot_of(level, half):
    _, core, at_x, at_y = position()
    slab = (level & 7) * 2 + half
    by_x, by_y = ((slab >> 2) - at_x) & 3, ((slab & 3) - at_y) & 3
    first = jnp.where(core == 0, by_y, by_x)
    second = jnp.where(core == 0, by_x, by_y)
    first = jnp.where(first == 3, 1, first + jnp.minimum(first, 1))
    second = jnp.where(second == 3, 1, second + jnp.minimum(second, 1))
    return second * 4 + first


NEAR = 12


def column_kernel(*refs):
    tall, out_ref = refs[:-1], refs[-1]
    z = position()[0]
    for half in range(HALVES):
        for level, offset in enumerate(LEVELS):
            out_ref[slot_of(z + offset, half)] = tall[level][half]
        out_ref[slot_of(z + 4, half)] = jnp.zeros((ROWS, ROWS), jnp.bfloat16)


def near_kernel(*refs):
    wide, b_buf, (total_ref, b_far_ref, a_far_ref) = refs[:3], refs[3], refs[4:]
    z = position()[0]
    for half in range(HALVES):
        slot = slot_of(z + 4, half)

        @pl.when(slot >= NEAR)
        def _():
            a_far_ref[half] = jnp.zeros(a_far_ref.shape[1:], jnp.bfloat16)

        for t in range(NEAR):

            @pl.when(slot == t)
            def _():
                a_far_ref[half] = wide[t // 4][t % 4]

    b_far_ref[...] = b_buf[NEAR:]
    for group in range(3):
        rows = b_buf[4 * group : 4 * group + 4].reshape(4 * ROWS, ROWS)
        for half in range(HALVES):
            product = jnp.dot(
                jnp.concatenate([wide[group][i, half] for i in range(4)], axis=1),
                rows,
                preferred_element_type=jnp.float32,
            )
            if group == 0:
                total_ref[half] = product
            else:
                total_ref[half] += product


def purify_kernel(
    branch_ref,
    pattern_ref,
    other_pattern_ref,
    block_ref,
    line_low,
    line_high,
    z_low,
    z_high,
    total_ref,
    b_far_ref,
    a_far_ref,
    ham_ref,
    other_ham_ref,
    atom_ref,
    other_atom_ref,
    overlap_ref,
    out_ref,
    give_ref,
    sums_ref,
    b_buf,
    done,
    out_sem,
):
    z, core, _, _ = position()
    b_buf[: SLABS - NEAR] = b_far_ref[...]
    for half, piece in enumerate((z_low, z_high)):
        slot = slot_of(z + 4, half)
        b_buf[SLABS - NEAR + half] = piece[...]

        @pl.when(slot >= NEAR)
        def _():
            b_buf[slot - NEAR] = piece[...]

    rows = b_buf[...].reshape((SLABS - NEAR + 2) * ROWS, ROWS)
    for half in range(HALVES):
        lead = line_low if half == 0 else line_high
        columns = [lead[i] for i in range(4)] + [a_far_ref[i, half] for i in range(2)]
        square = total_ref[half] + jnp.dot(
            jnp.concatenate(columns, axis=1), rows, preferred_element_type=jnp.float32
        )
        flip = branch_ref[core] == 1
        raw = jnp.where(flip, 2.0 * block_ref[half].astype(jnp.float32) - square, square)
        for i in range(3):
            for j in range(3):
                weight = jnp.where(core == half, pattern_ref[i, j], other_pattern_ref[i, j])
                at = (slice(i * TILE, (i + 1) * TILE), slice(j * TILE, (j + 1) * TILE))
                done[(half,) + at] = (raw[at] * weight.astype(jnp.float32)).astype(jnp.bfloat16)
    out_copy = pltpu.make_async_copy(done.at[core], out_ref.at[core], out_sem)
    out_copy.start()
    mine = terms_of(done[core].astype(jnp.float32), ham_ref, one_hot_of(atom_ref))
    theirs = done[1 - core]
    give_ref[...] = theirs
    theirs = terms_of(theirs.astype(jnp.float32), other_ham_ref, one_hot_of(other_atom_ref))
    zero = [jnp.where(core == 0, a, b) for a, b in zip(mine, theirs)]
    one = [jnp.where(core == 0, b, a) for a, b in zip(mine, theirs)]
    sums = overlap_ref[...] + by_line(zero, one, -2.0)
    for part in range(SLABS):
        sums_ref[part] = sums
    out_copy.wait()


def norm_kernel(parts_ref, velocities_ref, masses_ref, all_ref):
    sums = parts_ref[0]
    for part in range(1, parts_ref.shape[0]):
        sums = sums + parts_ref[part]
    speeds = velocities_ref[...]
    atoms = masses_ref.shape[1]
    for part in range(all_ref.shape[0]):
        all_ref[part] = sums
        all_ref[part, 6:7, :] = jnp.ones((1, LANES), jnp.float32)
        all_ref[part, 6:7, :atoms] = masses_ref[...]
        all_ref[part, 7:8, :] = jnp.broadcast_to(jnp.sum(speeds * speeds), (1, LANES))


def update_kernel(
    got_ref,
    half_ref,
    all_ref,
    positions_ref,
    velocities_ref,
    masses_ref,
    out_ref,
    forces_ref,
    speeds_ref,
    places_ref,
    out_sem,
):
    del half_ref
    z, core, _, _ = position()
    out_copy = pltpu.make_async_copy(got_ref, out_ref.at[1 - core], out_sem)
    out_copy.start()
    squares = jnp.zeros((3, LANES), jnp.float32)
    speed_norm = jnp.zeros((1, 1), jnp.float32)
    for level in range(all_ref.shape[0] // 2):
        zero, one = all_ref[2 * level], all_ref[2 * level + 1]
        both = zero + one
        for half, mass in enumerate((zero[6:7], one[6:7])):
            scaled = both[3 * half : 3 * half + 3] / jnp.sqrt(mass)
            squares = squares + scaled * scaled
        speed_norm = speed_norm + zero[7:8, 0:1] + one[7:8, 0:1]
    force_norm = jnp.sum(squares)
    both = all_ref[2 * z] + all_ref[2 * z + 1]
    forces = jnp.where(core == 0, both[0:3], both[3:6])[:, : forces_ref.shape[1]]
    forces_ref[...] = forces
    root_mass = jnp.sqrt(masses_ref[...])
    scaled = forces / root_mass
    speeds = (
        (1.0 - mixing) * velocities_ref[...]
        + mixing * jnp.sqrt(speed_norm) * scaled / jnp.sqrt(force_norm + epsilon)
        + time_step * scaled
    )
    speeds_ref[...] = speeds
    places_ref[...] = positions_ref[...] + time_step * speeds / root_mass
    out_copy.wait()


SMEM = pl.BlockSpec(memory_space=pltpu.SMEM)
VMEM = pl.BlockSpec(memory_space=pltpu.VMEM)
HBM = pl.BlockSpec(memory_space=pltpu.HBM)

def cost(slots):
    return pl.CostEstimate(
        flops=4 * ROWS * ROWS * ROWS * slots,
        bytes_accessed=8 * ROWS * ROWS * slots,
        transcendentals=0,
    )


PARAMS = pltpu.CompilerParams(vmem_limit_bytes=12 * 1024 * 1024)
LITTLE = pltpu.CompilerParams(vmem_limit_bytes=2 * 1024 * 1024)


def small(shape):
    return jax.ShapeDtypeStruct(shape, jnp.float32)


def local(
    density,
    weighted,
    ham_deriv,
    ovl_deriv,
    tile_pattern,
    branch,
    orbital_atom,
    positions,
    velocities,
    masses,
):
    give = pl.pallas_call(
        give_kernel,
        out_shape=jax.ShapeDtypeStruct((ROWS, ROWS), jnp.bfloat16),
        in_specs=[HBM],
        out_specs=VMEM,
        scratch_shapes=[pltpu.SemaphoreType.DMA],
        compiler_params=LITTLE,
    )(density)
    block = pl.pallas_call(
        block_kernel,
        out_shape=jax.ShapeDtypeStruct((HALVES, ROWS, ROWS), jnp.bfloat16),
        in_specs=[HBM, VMEM],
        out_specs=VMEM,
        scratch_shapes=[pltpu.SemaphoreType.DMA((2,))],
        compiler_params=LITTLE,
    )(density, send(give, core_swap()))
    first, last, columns, opposite = gather(block)

    other_ham = send(ham_deriv, core_swap())
    other_atom = send(orbital_atom, core_swap())
    other_pattern = send(tile_pattern, core_swap())

    overlap = pl.pallas_call(
        overlap_kernel,
        out_shape=small((8, LANES)),
        in_specs=[VMEM] * 3,
        out_specs=VMEM,
        compiler_params=pltpu.CompilerParams(vmem_limit_bytes=4 * 1024 * 1024),
    )(orbital_atom, weighted, ovl_deriv)

    total, b_far, a_far = pl.pallas_call(
        near_kernel,
        out_shape=(
            small((HALVES, ROWS, ROWS)),
            jax.ShapeDtypeStruct((SLABS - NEAR, ROWS, ROWS), jnp.bfloat16),
            jax.ShapeDtypeStruct((2, HALVES, ROWS, ROWS), jnp.bfloat16),
        ),
        in_specs=[VMEM] * 4,
        out_specs=(VMEM,) * 3,
        compiler_params=PARAMS,
        cost_estimate=cost(NEAR),
    )(*first, columns)
    half, give, sums = pl.pallas_call(
        purify_kernel,
        out_shape=(
            jax.ShapeDtypeStruct((2, ROWS, ROWS), jnp.bfloat16),
            jax.ShapeDtypeStruct((ROWS, ROWS), jnp.bfloat16),
            small((SLABS, 8, LANES)),
        ),
        in_specs=[SMEM] * 3 + [VMEM] * 13,
        out_specs=(HBM, VMEM, VMEM),
        scratch_shapes=[
            pltpu.VMEM((SLABS - NEAR + 2, ROWS, ROWS), jnp.bfloat16),
            pltpu.VMEM((HALVES, ROWS, ROWS), jnp.bfloat16),
            pltpu.SemaphoreType.DMA,
        ],
        compiler_params=PARAMS,
        cost_estimate=cost(SLABS - NEAR + 2),
    )(
        branch,
        tile_pattern,
        other_pattern,
        block,
        *last,
        *opposite,
        total,
        b_far,
        a_far,
        ham_deriv,
        other_ham,
        orbital_atom,
        other_atom,
        overlap,
    )
    got = send(give, core_swap())

    parts = lax.all_to_all(sums, "col", 0, 0)
    mass_row = masses[None, :]
    parts = pl.pallas_call(
        norm_kernel,
        out_shape=small((SLABS, 8, LANES)),
        in_specs=[VMEM] * 3,
        out_specs=VMEM,
        compiler_params=LITTLE,
    )(parts, velocities, mass_row)
    parts = lax.all_to_all(parts, "row", 0, 0)
    purified, forces, new_velocities, new_positions = pl.pallas_call(
        update_kernel,
        out_shape=(jax.ShapeDtypeStruct((2, ROWS, ROWS), jnp.bfloat16),)
        + (small(positions.shape),) * 3,
        in_specs=[HBM, HBM] + [VMEM] * 4,
        out_specs=(HBM, VMEM, VMEM, VMEM),
        scratch_shapes=[pltpu.SemaphoreType.DMA],
        input_output_aliases={1: 0},
        compiler_params=LITTLE,
    )(got, half, parts, positions, velocities, mass_row)
    return (purified, forces, new_velocities, new_positions)


def solution(mesh):
    in_specs = (
        P(None, "row", "col"),
        P("row", "col"),
        P(None, "row", "col"),
        P(None, "row", "col"),
        P("row", "col"),
        P(),
        P("row", None),
        P(None, "row"),
        P(None, "row"),
        P("row"),
    )
    out_specs = (P(None, "row", "col"), P(None, "row"), P(None, "row"), P(None, "row"))
    return jax.shard_map(local, mesh=mesh, in_specs=in_specs, out_specs=out_specs, check_vma=False)
```

```python
import jax
import jax.numpy as jnp
from jax import lax
from jax.experimental import pallas as pl
from jax.experimental.pallas import tpu as pltpu
from jax.sharding import PartitionSpec as P

TILE = 128
ROWS = 384
SLABS = 16
HALVES = 2
LANES = 128

mixing = 0.25
time_step = 0.1
epsilon = 1e-06

AXES = ("row", "col")


def place(z, core, x, y):
    return (z % 8 * 2 + core) * 16 + x % 4 * 4 + y % 4


def pairs(move):
    out = []
    for z in range(8):
        for core in range(2):
            for x in range(4):
                for y in range(4):
                    out.append((place(z, core, x, y), place(*move(z, core, x, y))))
    return out


def first_by(k):
    return pairs(lambda z, core, x, y: (z, core, x + k * core, y + k * (1 - core)))


def second_by(k):
    return pairs(lambda z, core, x, y: (z, core, x + k * (1 - core), y + k * core))


def z_by(k):
    return pairs(lambda z, core, x, y: (z + k, core, x, y))


def core_swap():
    return pairs(lambda z, core, x, y: (z, 1 - core, x, y))


def send(value, table):
    return lax.ppermute(value, AXES, table)


def after(value, *others):
    return lax.optimization_barrier((value,) + others)[0]


EARLY = 3 << 32


def gather(block):
    z_back = send(block, z_by(1))
    z_fore = send(block, z_by(-1))
    back = send(block, first_by(1))
    fore = send(block, first_by(-1))
    far = send(block, first_by(2))
    line = jnp.stack([block, back, fore, far])
    line_back = send(line, second_by(1))
    line_fore = send(line, second_by(-1))
    z_back_two = send(z_back, z_by(1))
    z_fore_two = send(z_fore, z_by(-1))
    z_back_three = send(z_back_two, z_by(1))
    z_fore_three = send(z_fore_two, z_by(-1))
    levels = (block, z_back, z_back_two, z_back_three, z_fore_three, z_fore_two, z_fore)
    columns = pl.pallas_call(
        column_kernel,
        out_shape=jax.ShapeDtypeStruct((SLABS, ROWS, ROWS), jnp.bfloat16),
        in_specs=[VMEM] * 7,
        out_specs=VMEM,
        compiler_params=LITTLE,
        cost_estimate=pl.CostEstimate(flops=EARLY, bytes_accessed=1 << 22, transcendentals=0),
    )(*levels)
    low, high = after((line_back[:, 0], line_fore[:, 1]), columns)
    line_low = send(low, second_by(1))
    line_high = send(high, second_by(-1))
    z_low = send(z_back_three[0], z_by(1))
    z_high = send(z_fore_three[1], z_by(-1))
    return (line, line_back, line_fore), (line_low, line_high), columns, (z_low, z_high)


LEVELS = (0, -1, -2, -3, 3, 2, 1)


def position():
    row, column = lax.axis_index("row"), lax.axis_index("col")
    return row >> 1, row & 1, column >> 2, column & 3


def terms_of(matrix, deriv_ref, one_hot):
    rows = []
    for x in range(3):
        column = jnp.sum(matrix * deriv_ref[x].astype(jnp.float32), axis=1, keepdims=True)
        rows.append(jnp.sum(column * one_hot, axis=0, keepdims=True))
    return rows


def one_hot_of(atom_ref):
    atoms = jnp.broadcast_to(atom_ref[...].astype(jnp.float32), (LANES, ROWS))
    lanes = lax.broadcasted_iota(jnp.int32, (ROWS, LANES), 1).astype(jnp.float32)
    return (jnp.transpose(atoms) == lanes).astype(jnp.float32)


def by_line(zero, one, scale):
    lines = lax.broadcasted_iota(jnp.int32, (8, LANES), 0)
    out = jnp.zeros((8, LANES), jnp.float32)
    for x in range(3):
        out = jnp.where(lines == x, scale * zero[x], out)
        out = jnp.where(lines == 3 + x, scale * one[x], out)
    return out


def overlap_kernel(atom_ref, weighted_ref, ovl_ref, out_ref):
    rows = terms_of(weighted_ref[...].astype(jnp.float32), ovl_ref, one_hot_of(atom_ref))
    lines = lax.broadcasted_iota(jnp.int32, (8, LANES), 0)
    own = (lines >= 3) == (position()[1] == 1)
    out_ref[...] = jnp.where(own, by_line(rows, rows, 2.0), 0.0)


def give_kernel(density_ref, give_ref, sem):
    core = position()[1]
    copy = pltpu.make_async_copy(density_ref.at[1 - core], give_ref, sem)
    copy.start()
    copy.wait()


def block_kernel(density_ref, got_ref, block_ref, sems):
    core = position()[1]
    mine = pltpu.make_async_copy(density_ref.at[core], block_ref.at[core], sems.at[0])
    theirs = pltpu.make_async_copy(got_ref, block_ref.at[1 - core], sems.at[1])
    mine.start()
    theirs.start()
    mine.wait()
    theirs.wait()


def slot_of(level, half):
    _, core, at_x, at_y = position()
    slab = (level & 7) * 2 + half
    by_x, by_y = ((slab >> 2) - at_x) & 3, ((slab & 3) - at_y) & 3
    first = jnp.where(core == 0, by_y, by_x)
    second = jnp.where(core == 0, by_x, by_y)
    first = jnp.where(first == 3, 1, first + jnp.minimum(first, 1))
    second = jnp.where(second == 3, 1, second + jnp.minimum(second, 1))
    return second * 4 + first


NEAR = 12


def column_kernel(*refs):
    tall, out_ref = refs[:-1], refs[-1]
    z = position()[0]
    for half in range(HALVES):
        for level, offset in enumerate(LEVELS):
            out_ref[slot_of(z + offset, half)] = tall[level][half]
        out_ref[slot_of(z + 4, half)] = jnp.zeros((ROWS, ROWS), jnp.bfloat16)


def near_kernel(*refs):
    wide, b_buf, (total_ref, b_far_ref, a_far_ref) = refs[:3], refs[3], refs[4:]
    z = position()[0]
    for half in range(HALVES):
        slot = slot_of(z + 4, half)

        @pl.when(slot >= NEAR)
        def _():
            a_far_ref[half] = jnp.zeros(a_far_ref.shape[1:], jnp.bfloat16)

        for t in range(NEAR):

            @pl.when(slot == t)
            def _():
                a_far_ref[half] = wide[t // 4][t % 4]

    b_far_ref[...] = b_buf[NEAR:]
    for group in range(3):
        rows = b_buf[4 * group : 4 * group + 4].reshape(4 * ROWS, ROWS)
        for half in range(HALVES):
            product = jnp.dot(
                jnp.concatenate([wide[group][i, half] for i in range(4)], axis=1),
                rows,
                preferred_element_type=jnp.float32,
            )
            if group == 0:
                total_ref[half] = product
            else:
                total_ref[half] += product


def opposite_kernel(z_low, z_high, part_ref, b_far_ref, a_far_ref, total_ref, b_last_ref):
    z = position()[0]
    b_last_ref[...] = b_far_ref[...]
    for half, piece in enumerate((z_low, z_high)):
        slot = slot_of(z + 4, half)

        @pl.when(slot >= NEAR)
        def _():
            b_last_ref[slot - NEAR] = piece[...]

    rows = jnp.concatenate([z_low[...], z_high[...]], axis=0)
    for half in range(HALVES):
        columns = jnp.concatenate([a_far_ref[i, half] for i in range(2)], axis=1)
        total_ref[half] = part_ref[half] + jnp.dot(
            columns, rows, preferred_element_type=jnp.float32
        )


def purify_kernel(
    branch_ref,
    pattern_ref,
    other_pattern_ref,
    block_ref,
    line_low,
    line_high,
    total_ref,
    b_last_ref,
    ham_ref,
    other_ham_ref,
    atom_ref,
    other_atom_ref,
    overlap_ref,
    out_ref,
    give_ref,
    sums_ref,
    done,
    out_sem,
):
    core = position()[1]
    rows = b_last_ref[...].reshape((SLABS - NEAR) * ROWS, ROWS)
    for half in range(HALVES):
        lead = line_low if half == 0 else line_high
        columns = [lead[i] for i in range(4)]
        square = total_ref[half] + jnp.dot(
            jnp.concatenate(columns, axis=1), rows, preferred_element_type=jnp.float32
        )
        flip = branch_ref[core] == 1
        raw = jnp.where(flip, 2.0 * block_ref[half].astype(jnp.float32) - square, square)
        for i in range(3):
            for j in range(3):
                weight = jnp.where(core == half, pattern_ref[i, j], other_pattern_ref[i, j])
                at = (slice(i * TILE, (i + 1) * TILE), slice(j * TILE, (j + 1) * TILE))
                done[(half,) + at] = (raw[at] * weight.astype(jnp.float32)).astype(jnp.bfloat16)
    out_copy = pltpu.make_async_copy(done.at[core], out_ref.at[core], out_sem)
    out_copy.start()
    mine = terms_of(done[core].astype(jnp.float32), ham_ref, one_hot_of(atom_ref))
    theirs = done[1 - core]
    give_ref[...] = theirs
    theirs = terms_of(theirs.astype(jnp.float32), other_ham_ref, one_hot_of(other_atom_ref))
    zero = [jnp.where(core == 0, a, b) for a, b in zip(mine, theirs)]
    one = [jnp.where(core == 0, b, a) for a, b in zip(mine, theirs)]
    sums = overlap_ref[...] + by_line(zero, one, -2.0)
    for part in range(SLABS):
        sums_ref[part] = sums
    out_copy.wait()


def norm_kernel(parts_ref, velocities_ref, masses_ref, all_ref):
    sums = parts_ref[0]
    for part in range(1, parts_ref.shape[0]):
        sums = sums + parts_ref[part]
    speeds = velocities_ref[...]
    atoms = masses_ref.shape[1]
    for part in range(all_ref.shape[0]):
        all_ref[part] = sums
        all_ref[part, 6:7, :] = jnp.ones((1, LANES), jnp.float32)
        all_ref[part, 6:7, :atoms] = masses_ref[...]
        all_ref[part, 7:8, :] = jnp.broadcast_to(jnp.sum(speeds * speeds), (1, LANES))


def update_kernel(
    got_ref,
    half_ref,
    all_ref,
    positions_ref,
    velocities_ref,
    masses_ref,
    out_ref,
    forces_ref,
    speeds_ref,
    places_ref,
    out_sem,
):
    del half_ref
    z, core, _, _ = position()
    out_copy = pltpu.make_async_copy(got_ref, out_ref.at[1 - core], out_sem)
    out_copy.start()
    squares = jnp.zeros((3, LANES), jnp.float32)
    speed_norm = jnp.zeros((1, 1), jnp.float32)
    for level in range(all_ref.shape[0] // 2):
        zero, one = all_ref[2 * level], all_ref[2 * level + 1]
        both = zero + one
        for half, mass in enumerate((zero[6:7], one[6:7])):
            scaled = both[3 * half : 3 * half + 3] / jnp.sqrt(mass)
            squares = squares + scaled * scaled
        speed_norm = speed_norm + zero[7:8, 0:1] + one[7:8, 0:1]
    force_norm = jnp.sum(squares)
    both = all_ref[2 * z] + all_ref[2 * z + 1]
    forces = jnp.where(core == 0, both[0:3], both[3:6])[:, : forces_ref.shape[1]]
    forces_ref[...] = forces
    root_mass = jnp.sqrt(masses_ref[...])
    scaled = forces / root_mass
    speeds = (
        (1.0 - mixing) * velocities_ref[...]
        + mixing * jnp.sqrt(speed_norm) * scaled / jnp.sqrt(force_norm + epsilon)
        + time_step * scaled
    )
    speeds_ref[...] = speeds
    places_ref[...] = positions_ref[...] + time_step * speeds / root_mass
    out_copy.wait()


SMEM = pl.BlockSpec(memory_space=pltpu.SMEM)
VMEM = pl.BlockSpec(memory_space=pltpu.VMEM)
HBM = pl.BlockSpec(memory_space=pltpu.HBM)

def cost(slots):
    return pl.CostEstimate(
        flops=4 * ROWS * ROWS * ROWS * slots,
        bytes_accessed=8 * ROWS * ROWS * slots,
        transcendentals=0,
    )


PARAMS = pltpu.CompilerParams(vmem_limit_bytes=12 * 1024 * 1024)
LITTLE = pltpu.CompilerParams(vmem_limit_bytes=2 * 1024 * 1024)


def small(shape):
    return jax.ShapeDtypeStruct(shape, jnp.float32)


def local(
    density,
    weighted,
    ham_deriv,
    ovl_deriv,
    tile_pattern,
    branch,
    orbital_atom,
    positions,
    velocities,
    masses,
):
    give = pl.pallas_call(
        give_kernel,
        out_shape=jax.ShapeDtypeStruct((ROWS, ROWS), jnp.bfloat16),
        in_specs=[HBM],
        out_specs=VMEM,
        scratch_shapes=[pltpu.SemaphoreType.DMA],
        compiler_params=LITTLE,
    )(density)
    block = pl.pallas_call(
        block_kernel,
        out_shape=jax.ShapeDtypeStruct((HALVES, ROWS, ROWS), jnp.bfloat16),
        in_specs=[HBM, VMEM],
        out_specs=VMEM,
        scratch_shapes=[pltpu.SemaphoreType.DMA((2,))],
        compiler_params=LITTLE,
    )(density, send(give, core_swap()))
    first, last, columns, opposite = gather(block)

    other_ham = send(ham_deriv, core_swap())
    other_atom = send(orbital_atom, core_swap())
    other_pattern = send(tile_pattern, core_swap())

    overlap = pl.pallas_call(
        overlap_kernel,
        out_shape=small((8, LANES)),
        in_specs=[VMEM] * 3,
        out_specs=VMEM,
        compiler_params=pltpu.CompilerParams(vmem_limit_bytes=4 * 1024 * 1024),
    )(orbital_atom, weighted, ovl_deriv)

    total, b_far, a_far = pl.pallas_call(
        near_kernel,
        out_shape=(
            small((HALVES, ROWS, ROWS)),
            jax.ShapeDtypeStruct((SLABS - NEAR, ROWS, ROWS), jnp.bfloat16),
            jax.ShapeDtypeStruct((2, HALVES, ROWS, ROWS), jnp.bfloat16),
        ),
        in_specs=[VMEM] * 4,
        out_specs=(VMEM,) * 3,
        compiler_params=PARAMS,
        cost_estimate=cost(NEAR),
    )(*first, columns)
    total, b_last = pl.pallas_call(
        opposite_kernel,
        out_shape=(
            small((HALVES, ROWS, ROWS)),
            jax.ShapeDtypeStruct((SLABS - NEAR, ROWS, ROWS), jnp.bfloat16),
        ),
        in_specs=[VMEM] * 5,
        out_specs=(VMEM, VMEM),
        compiler_params=PARAMS,
        cost_estimate=cost(2),
    )(*opposite, total, b_far, a_far)
    half, give, sums = pl.pallas_call(
        purify_kernel,
        out_shape=(
            jax.ShapeDtypeStruct((2, ROWS, ROWS), jnp.bfloat16),
            jax.ShapeDtypeStruct((ROWS, ROWS), jnp.bfloat16),
            small((SLABS, 8, LANES)),
        ),
        in_specs=[SMEM] * 3 + [VMEM] * 10,
        out_specs=(HBM, VMEM, VMEM),
        scratch_shapes=[
            pltpu.VMEM((HALVES, ROWS, ROWS), jnp.bfloat16),
            pltpu.SemaphoreType.DMA,
        ],
        compiler_params=PARAMS,
        cost_estimate=cost(SLABS - NEAR),
    )(
        branch,
        tile_pattern,
        other_pattern,
        block,
        *last,
        total,
        b_last,
        ham_deriv,
        other_ham,
        orbital_atom,
        other_atom,
        overlap,
    )
    got = send(give, core_swap())

    parts = lax.all_to_all(sums, "col", 0, 0)
    mass_row = masses[None, :]
    parts = pl.pallas_call(
        norm_kernel,
        out_shape=small((SLABS, 8, LANES)),
        in_specs=[VMEM] * 3,
        out_specs=VMEM,
        compiler_params=LITTLE,
    )(parts, velocities, mass_row)
    parts = lax.all_to_all(parts, "row", 0, 0)
    purified, forces, new_velocities, new_positions = pl.pallas_call(
        update_kernel,
        out_shape=(jax.ShapeDtypeStruct((2, ROWS, ROWS), jnp.bfloat16),)
        + (small(positions.shape),) * 3,
        in_specs=[HBM, HBM] + [VMEM] * 4,
        out_specs=(HBM, VMEM, VMEM, VMEM),
        scratch_shapes=[pltpu.SemaphoreType.DMA],
        input_output_aliases={1: 0},
        compiler_params=LITTLE,
    )(got, half, parts, positions, velocities, mass_row)
    return (purified, forces, new_velocities, new_positions)


def solution(mesh):
    in_specs = (
        P(None, "row", "col"),
        P("row", "col"),
        P(None, "row", "col"),
        P(None, "row", "col"),
        P("row", "col"),
        P(),
        P("row", None),
        P(None, "row"),
        P(None, "row"),
        P("row"),
    )
    out_specs = (P(None, "row", "col"), P(None, "row"), P(None, "row"), P(None, "row"))
    return jax.shard_map(local, mesh=mesh, in_specs=in_specs, out_specs=out_specs, check_vma=False)
```
